32 devices in a mesh: grp: 4 (over y, x), dev: 8 (over z, core).
Axes of the slice: x: 2, y: 2, z: 4, core: 2. Of those that a mesh axis runs over, the one named last changes fastest.
Arguments:
- cache_k: bfloat16 [64, 8, 256, 128], P('grp', None, 'dev')
- cache_v: bfloat16 [64, 8, 256, 128], P('grp', None, 'dev'), may hold values from -6 to 6
- source: int32 [64], replicated, may hold values from 0 to 63, as said below
- lengths: int32 [64], P('grp'), may hold values from 1 to 255
- query: bfloat16 [64, 6144], P('grp')
- new_key: bfloat16 [64, 8, 128], P('grp'), may hold values from -6 to 6
- new_value: bfloat16 [64, 8, 128], P('grp'), may hold values from -6 to 6
- resid: bfloat16 [64, 6144], P('grp', 'dev'), may hold values from -6 to 6
- out_weight: bfloat16 [6144, 6144], P('dev'), may hold values from -0.078125 to 0.078125
- norm_gain: bfloat16 [6144], replicated, may hold values from 0.099609375 to 1.8984375
- w_gate: bfloat16 [6144, 65536], P(None, ('grp', 'dev')), may hold values from -0.078125 to 0.078125
- w_up: bfloat16 [6144, 65536], P(None, ('grp', 'dev')), may hold values from -0.078125 to 0.078125
- w_down: bfloat16 [65536, 6144], P(('grp', 'dev')), may hold values from -0.0625 to 0.0625
- expert_ids: int32 [64, 2], P('grp'), may hold values from 0 to 7, all different within a row; in each aligned block of 16 rows (0 to 15, 16 to 31, ...) at most 8 rows name the same one
- gate_codes: int32 [64, 2], P('grp'), may hold values from 1 to 1023
Outputs:
- new_cache_k: bfloat16 [64, 8, 256, 128], P('grp', None, 'dev')
- new_cache_v: bfloat16 [64, 8, 256, 128], P('grp', None, 'dev')
- layer_out: bfloat16 [64, 6144], P('grp', 'dev')
The draws below stay inside these ranges and needn't reach their ends.
Inputs may be any that keep to these rules, and one draw needn't show every extreme that they name: source is a permutation of the 64 slots; each group of 16 slots sends exactly 2 of its requests to each other group and receives exactly 2 from each other group into the slots it vacated; every other slot keeps its own request. `expert_ids`: in the 16 rows of each group no expert is named more than 8 times.
All inputs are finite; a program needn't handle non-finite values.
Results may differ from the reference program's by a relative error of at most 0.012.
Values may be sent and summed in bfloat16 or wider, within the bound.
A program may use at most 128 MiB of HBM per device.

```python
import math
import jax
import jax.numpy as jnp
import numpy as np
from jax import lax

D = 6144
HEADS = 48
KV_HEADS = 8
HEAD_DIM = 128
EXPERTS = 8
FF = 8192
TOP = 2
REQ_G = 16
GQ = 6
LEN = 256
REQS = 64
MOVE = 2
CAP = 8


def align_pattern(key):
    base = jax.random.fold_in(key, 7)
    magnitude = jax.random.uniform(jax.random.fold_in(base, 1), (KV_HEADS, HEAD_DIM), jnp.float32, 2.8, 3.0)
    flips = jax.random.bernoulli(jax.random.fold_in(base, 2), 0.5, (KV_HEADS, HEAD_DIM))
    return jnp.where(flips, magnitude, -magnitude)


def draw_query(key, part):
    shape = (REQS, HEADS * HEAD_DIM)
    values = jax.random.normal(jax.random.fold_in(key, 11), shape, jnp.float32)
    pattern = align_pattern(key)
    strength = jax.random.uniform(jax.random.fold_in(key, 13), (REQS,), jnp.float32, 1.5, 6.0)
    chosen = jax.random.uniform(jax.random.fold_in(key, 14), (REQS,), jnp.float32) < 0.3
    aligned = jnp.broadcast_to(pattern[None, :, None, :], (REQS, KV_HEADS, GQ, HEAD_DIM)) * strength[:, None, None, None]
    values = jnp.where(chosen[:, None], aligned.reshape(shape), values)
    return values.astype(jnp.bfloat16)


def draw_cache_k(key, part):
    shape = (REQS, KV_HEADS, LEN, HEAD_DIM)
    values = jax.random.normal(jax.random.fold_in(key, 17), shape, jnp.float32)
    pattern = align_pattern(key)
    positions = jnp.arange(LEN)[None, None, :, None]
    first = jnp.broadcast_to(pattern[None, :, None, :], shape)
    values = jnp.where(positions == 0, first, values)
    values = jnp.where(positions == 1, first * 0.99, values)
    return values.astype(jnp.bfloat16)


def draw_source(key, part):
    group_count = REQS // REQ_G
    leave_count = MOVE * (group_count - 1)
    groups = jnp.arange(group_count, dtype=jnp.int32)

    def shuffle_of(group):
        return jax.random.permutation(jax.random.fold_in(jax.random.fold_in(key, 22), group), REQ_G).astype(jnp.int32)
    shuffled = jax.vmap(shuffle_of)(groups)
    leave_range = jnp.arange(leave_count, dtype=jnp.int32)
    from_group = (groups[:, None] - 1 - leave_range[None, :] // MOVE) % group_count
    from_slot = shuffled[from_group, jnp.broadcast_to(leave_range[None, :], (group_count, leave_count))]
    stays = groups[:, None] * REQ_G + jnp.arange(REQ_G, dtype=jnp.int32)[None, :]
    target_rows = jnp.broadcast_to(groups[:, None], (group_count, leave_count))
    result = stays.at[target_rows, shuffled[:, :leave_count]].set(from_group * REQ_G + from_slot)
    return result.reshape(-1).astype(jnp.int32)


def set_ends(drawn, own_key, low, largest):
    dims = drawn.shape
    index_at = [jax.random.randint(jax.random.fold_in(own_key, axis), (), 0, dims[axis]) for axis in range(len(dims))]
    drawn = drawn.at[tuple(index_at)].set(low)
    longest = dims.index(max(dims))
    index_at[longest] = (index_at[longest] + 1) % dims[longest]
    return drawn.at[tuple(index_at)].set(largest)


def shard_levels(own_key, extent, shards, low, top_value):
    def one(dim, blocks):
        heights = jax.random.uniform(jax.random.fold_in(jax.random.fold_in(own_key, 6), dim), (blocks,), jnp.float32, low / len(shards), top_value / len(shards))
        return jnp.repeat(jnp.exp(heights), extent[dim] // blocks).reshape((-1,) + (1,) * (len(extent) - dim - 1))

    factor_of = one(*shards[0])
    for cut in shards[1:]:
        factor_of = factor_of * one(*cut)
    return factor_of


def shared_out(rng, own, number, rows, amount, top, reach, skew):
    ranking = jax.random.permutation(rng, amount)
    packed, usual = load_shares(amount, rows * top, reach, skew, True), load_shares(amount, rows * top, reach, skew, False)
    places = jnp.arange(amount)

    def named(sizes, offset_by):
        used = int((sizes > 0).sum())
        fixed = max(1, used // 4)
        shifted = fixed + (places - fixed + offset_by * (used - fixed)) % max(1, amount - fixed)
        return jnp.zeros((amount,), jnp.int32).at[ranking[jnp.where(places < fixed, places, shifted)]].set(jnp.asarray(sizes, jnp.int32))

    sizes = jnp.where(number % 4 == 0, named(packed, number // 4), named(usual, number - number // 4 - 1))
    mixed = jax.random.permutation(jax.random.fold_in(own, 3), amount)
    giver, sink = mixed[0:amount // 2 * 2:2], mixed[1:amount // 2 * 2:2]
    margin = jnp.minimum(sizes[giver] - 1, reach - sizes[sink]) // 2
    margin = jnp.where((giver == ranking[0]) | (sink == ranking[0]) | (sizes[sink] == 0), 0, jnp.maximum(margin, 0))
    shifted = jax.random.randint(jax.random.fold_in(own, 4), (amount // 2,), 0, 1 << 20) % (margin + 1)
    sizes = sizes.at[giver].add(-shifted).at[sink].add(shifted)
    members = jnp.searchsorted(jnp.cumsum(sizes), jnp.arange(rows * top), side="right").astype(jnp.int32)
    grid = members.reshape(top, rows).T
    grid = grid[jax.random.permutation(jax.random.fold_in(own, 1), rows)]
    offset_by = jax.random.randint(jax.random.fold_in(own, 2), (rows, 1), 0, top)
    return jnp.take_along_axis(grid, (jnp.arange(top)[None, :] + offset_by) % top, axis=1)


def load_shares(count, total, limit, lean, full):
    portions = [(1 << 20) // math.isqrt(grade ** lean) + 1 for grade in range(1, count + 1)]
    largest = limit if full else min(limit, max(-(-total // count), total * portions[0] // sum(portions)))
    least = 1 if total - largest >= count - 1 else 0
    holding, spare = [largest] + [least] * (count - 1), total - largest - least * (count - 1)
    while spare > 0:
        free = [i for i in range(1, count) if holding[i] < largest] or [i for i in range(1, count) if holding[i] < limit]
        whole, budget = sum([portions[i] for i in free]), spare
        for i in free:
            extra = min(limit - holding[i], max(1, budget * portions[i] // whole), spare)
            holding[i] = holding[i] + extra
            spare = spare - extra
    return np.array(holding)


def centred(rng, extent, scale, limit, split=(), held_as=jnp.bfloat16):
    values = scale * jax.random.normal(rng, extent, jnp.float32)
    if split:
        values = values * shard_levels(rng, extent, split, -0.22, 0.18)
    return jnp.clip(values, -limit, limit).astype(held_as)


def setup_inputs(seed: int = 0) -> dict:
    arg_keys = jax.random.split(jax.random.key(seed), 16)
    cache_k = draw_cache_k(jax.random.fold_in(arg_keys[15], 71), 0)
    cache_v = centred(arg_keys[1], (REQS, KV_HEADS, LEN, HEAD_DIM), 1.0, 6.0, ((0, 4), (2, 8)))
    source = draw_source(jax.random.fold_in(arg_keys[15], 71), 0)
    lengths = set_ends(jax.random.randint(arg_keys[3], (REQS,), 1, LEN), jax.random.fold_in(arg_keys[3], 1), 1, LEN - 1).astype(jnp.int32)
    query = draw_query(jax.random.fold_in(arg_keys[15], 71), 0)
    new_key = centred(arg_keys[5], (REQS, KV_HEADS, HEAD_DIM), 1.0, 6.0, ((0, 4),))
    new_value = centred(arg_keys[6], (REQS, KV_HEADS, HEAD_DIM), 1.0, 6.0, ((0, 4),))
    resid = centred(arg_keys[7], (REQS, D), 1.0, 6.0, ((0, 4), (1, 8)))
    out_weight = centred(arg_keys[8], (HEADS * HEAD_DIM, D), (HEADS * HEAD_DIM) ** -0.5, 0.078125, ((0, 8),))
    norm_gain = jnp.clip(1.0 + 0.18 * jax.random.normal(arg_keys[9], (D,), jnp.float32), 0.099609375, 1.8984375).astype(jnp.bfloat16)
    w_gate = centred(arg_keys[10], (D, EXPERTS * FF), D ** -0.5, 0.078125, ((1, 32),))
    w_up = centred(arg_keys[11], (D, EXPERTS * FF), D ** -0.5, 0.078125, ((1, 32),))
    w_down = centred(arg_keys[12], (EXPERTS * FF, D), FF ** -0.5, 0.0625, ((0, 32),))
    expert_ids_keys = jax.random.split(jax.random.fold_in(arg_keys[13], 1), REQS // REQ_G)
    expert_ids_turns = jax.random.permutation(jax.random.fold_in(arg_keys[13], 3), REQS // REQ_G)
    expert_ids = jax.vmap(lambda own, number: shared_out(jax.random.fold_in(arg_keys[13], 2), own, number, REQ_G, EXPERTS, TOP, CAP, 2))(expert_ids_keys, expert_ids_turns).reshape((REQS, TOP))
    gate_codes = set_ends(jax.random.randint(arg_keys[14], (REQS, TOP), 1, 1024), jax.random.fold_in(arg_keys[14], 1), 1, 1023).astype(jnp.int32)
    return dict(cache_k=cache_k, cache_v=cache_v, source=source, lengths=lengths, query=query, new_key=new_key, new_value=new_value, resid=resid, out_weight=out_weight, norm_gain=norm_gain, w_gate=w_gate, w_up=w_up, w_down=w_down, expert_ids=expert_ids, gate_codes=gate_codes)


def reference(cache_k, cache_v, source, lengths, query, new_key, new_value, resid, out_weight, norm_gain, w_gate, w_up, w_down, expert_ids, gate_codes):
    positions = jnp.arange(LEN, dtype=jnp.int32)
    hit = positions[None, :] == lengths[:, None]
    moved_k = jnp.take(cache_k, source, axis=0)
    moved_v = jnp.take(cache_v, source, axis=0)
    new_cache_k = jnp.where(hit[:, None, :, None], new_key[:, :, None, :], moved_k)
    new_cache_v = jnp.where(hit[:, None, :, None], new_value[:, :, None, :], moved_v)
    scale = 1.0 / HEAD_DIM ** 0.5

    def attend(items):
        keys, values, one_query, length = items
        grouped = one_query.astype(jnp.float32).reshape(KV_HEADS, GQ, HEAD_DIM)
        scores = jnp.einsum('kgh,kph->kgp', grouped, keys.astype(jnp.float32), precision=lax.Precision.HIGHEST) * scale
        valid = (positions <= length)[None, None, :]
        scores = jnp.where(valid, scores, jnp.float32(-1e+30))
        peak = lax.optimization_barrier(jnp.max(scores, axis=-1, keepdims=True))
        weights = jnp.where(valid, jnp.exp(scores - peak), jnp.float32(0.0))
        total = lax.optimization_barrier(jnp.sum(weights, axis=-1))
        context = jnp.einsum('kgp,kph->kgh', weights, values.astype(jnp.float32), precision=lax.Precision.HIGHEST)
        return (context / total[..., None]).reshape(HEADS * HEAD_DIM)
    attn = lax.map(attend, (new_cache_k, new_cache_v, query, lengths)).astype(jnp.bfloat16)
    mixed = resid.astype(jnp.float32) + jnp.dot(attn, out_weight, preferred_element_type=jnp.float32)
    mean_sq = lax.optimization_barrier(jnp.mean(mixed * mixed, axis=-1, keepdims=True))
    normed = (mixed * lax.rsqrt(mean_sq + 1e-05) * norm_gain.astype(jnp.float32)).astype(jnp.bfloat16)
    codes = gate_codes.astype(jnp.float32)
    gate_weight = codes / lax.optimization_barrier(jnp.sum(codes, axis=-1, keepdims=True))
    expert_range = jnp.arange(EXPERTS, dtype=jnp.int32)
    mixing = lax.optimization_barrier(jnp.sum(gate_weight[:, :, None] * (expert_ids[:, :, None] == expert_range[None, None, :]).astype(jnp.float32), axis=1))

    def run_expert(expert):
        start = (expert * FF).astype(jnp.int32)
        gate_cols = lax.dynamic_slice_in_dim(w_gate, start, FF, 1)
        up_cols = lax.dynamic_slice_in_dim(w_up, start, FF, 1)
        down_rows = lax.dynamic_slice_in_dim(w_down, start, FF, 0)
        gate_val = jnp.dot(normed, gate_cols, preferred_element_type=jnp.float32)
        up_val = jnp.dot(normed, up_cols, preferred_element_type=jnp.float32)
        hidden = (jax.nn.silu(gate_val) * up_val).astype(jnp.bfloat16)
        return jnp.dot(hidden, down_rows, preferred_element_type=jnp.float32)
    expert_out = lax.map(run_expert, expert_range)
    moe = lax.optimization_barrier(jnp.sum(mixing.T[:, :, None] * expert_out, axis=0))
    layer_out = (mixed + moe).astype(jnp.bfloat16)
    return (new_cache_k, new_cache_v, layer_out)
```

```python
import jax
import jax.numpy as jnp
from jax import lax
from jax.experimental import pallas as pl
from jax.experimental.pallas import tpu as pltpu
from jax.sharding import PartitionSpec as P

EXPERTS = 8
TOP = 2
MOVE = 2
CAP = 8


def joined(array, axis, combine):
    everything = jax.tree.map(
        lambda part, kind: lax.all_gather(part.astype(kind), axis),
        array,
        (jnp.bfloat16, jnp.bfloat16, jnp.bfloat16),
    )

    def take(k):
        return jax.tree.map(lambda part, own: part[k].astype(own.dtype), everything, array)

    return lax.fori_loop(
        1, lax.axis_size(axis), lambda k, so_far: combine(so_far, take(k)), take(0)
    )


def expert_ffn(rows, w_gate, w_up, w_down):
    gate_val = jnp.dot(rows, w_gate, preferred_element_type=jnp.float32)
    up_val = jnp.dot(rows, w_up, preferred_element_type=jnp.float32)
    hidden = (jax.nn.silu(gate_val) * up_val).astype(jnp.bfloat16)
    return jnp.dot(hidden, w_down, preferred_element_type=jnp.float32)


def merge_states(earlier, later):
    top = jnp.maximum(earlier[0], later[0])
    first_scale = jnp.exp(earlier[0] - top)
    second_scale = jnp.exp(later[0] - top)
    totals = earlier[1] * first_scale + later[1] * second_scale
    context = earlier[2] * first_scale[..., None] + later[2] * second_scale[..., None]
    return (top, totals, context)


def on_device(
    cache_k,
    cache_v,
    source,
    lengths,
    query,
    new_key,
    new_value,
    resid,
    out_weight,
    norm_gain,
    w_gate,
    w_up,
    w_down,
    expert_ids,
    gate_codes,
):
    group_count = lax.axis_size("grp")
    dev_count = lax.axis_size("dev")
    group_id = lax.axis_index("grp")
    dev_id = lax.axis_index("dev")
    per_group, kv_heads, block_len, head_dim = cache_k.shape
    all_slots = source.shape[0]
    model_width = resid.shape[1] * dev_count
    feat_width = resid.shape[1]
    slot_range = jnp.arange(all_slots, dtype=jnp.int32)
    inverse = jnp.sum(
        jnp.where(source[:, None] == slot_range[None, :], slot_range[:, None], 0), axis=0
    )
    old_group = slot_range // per_group
    dest_group = inverse // per_group
    leaving = dest_group != old_group
    same_route = (old_group[:, None] == old_group[None, :]) & (
        dest_group[:, None] == dest_group[None, :]
    )
    earlier_movers = same_route & leaving[None, :] & (slot_range[None, :] < slot_range[:, None])
    mover_rank = jnp.sum(earlier_movers.astype(jnp.int32), axis=1)
    first_slot = group_id * per_group
    my_leaving = lax.dynamic_slice_in_dim(leaving, first_slot, per_group)
    my_dest = lax.dynamic_slice_in_dim(dest_group, first_slot, per_group)
    my_rank = lax.dynamic_slice_in_dim(mover_rank, first_slot, per_group)
    buffer_range = jnp.arange(group_count * MOVE, dtype=jnp.int32)
    local_range = jnp.arange(per_group, dtype=jnp.int32)
    match = (
        my_leaving[None, :]
        & (my_dest[None, :] == (buffer_range // MOVE)[:, None])
        & (my_rank[None, :] == (buffer_range % MOVE)[:, None])
    )
    picked = jnp.sum(jnp.where(match, local_range[None, :], 0), axis=1)
    filled = jnp.any(match, axis=1)[:, None, None, None]
    zero_block = jnp.zeros((), jnp.bfloat16)
    send_k = jnp.where(filled, jnp.take(cache_k, picked, axis=0), zero_block)
    send_v = jnp.where(filled, jnp.take(cache_v, picked, axis=0), zero_block)
    recv_k, recv_v = (
        lax.all_to_all(send_k, "grp", split_axis=0, concat_axis=0, tiled=True),
        lax.all_to_all(send_v, "grp", split_axis=0, concat_axis=0, tiled=True),
    )
    my_source = lax.dynamic_slice_in_dim(source, first_slot, per_group)
    source_group = my_source // per_group
    arrival = per_group + source_group * MOVE + jnp.take(mover_rank, my_source)
    where_from = jnp.where(source_group == group_id, my_source - first_slot, arrival)
    moved_k = jnp.take(jnp.concatenate([cache_k, recv_k], axis=0), where_from, axis=0)
    moved_v = jnp.take(jnp.concatenate([cache_v, recv_v], axis=0), where_from, axis=0)
    positions = dev_id * block_len + jnp.arange(block_len, dtype=jnp.int32)
    hit = (positions[None, :] == lengths[:, None])[:, None, :, None]
    new_cache_k = jnp.where(hit, new_key[:, :, None, :], moved_k)
    new_cache_v = jnp.where(hit, new_value[:, :, None, :], moved_v)
    share_heads = query.shape[1] // (kv_heads * head_dim)
    grouped = query.reshape(per_group, kv_heads, share_heads, head_dim)
    scores = (
        jnp.einsum("rkgh,rkph->rkgp", grouped, new_cache_k, preferred_element_type=jnp.float32)
        / head_dim**0.5
    )
    valid = (positions[None, :] <= lengths[:, None])[:, None, None, :]
    scores = jnp.where(valid, scores, jnp.float32(-1e30))
    local_peak = jnp.max(scores, axis=-1)
    values_wide = new_cache_v.astype(jnp.float32)
    weights = jnp.where(valid, jnp.exp(scores - local_peak[..., None]), jnp.float32(0.0))
    local_total = jnp.sum(weights, axis=-1)
    local_context = jnp.einsum(
        "rkgp,rkph->rkgh", weights, values_wide, precision=lax.Precision.HIGHEST
    )
    peak, totals, context = joined((local_peak, local_total, local_context), "dev", merge_states)
    attn = (context / totals[..., None]).reshape(per_group, -1).astype(jnp.bfloat16)
    row_count = out_weight.shape[0]
    attn_mine = lax.dynamic_slice_in_dim(attn, dev_id * row_count, row_count, 1)
    partial_value = jnp.dot(attn_mine, out_weight, preferred_element_type=jnp.float32)
    expert_range = jnp.arange(EXPERTS, dtype=jnp.int32)
    onehot = expert_ids[:, :, None] == expert_range[None, None, :]
    flat_hot = onehot.reshape(per_group * TOP, EXPERTS).astype(jnp.int32)
    before = jnp.cumsum(flat_hot, axis=0) - flat_hot
    route_rank = jnp.sum(before * flat_hot, axis=1).reshape(per_group, TOP)
    slot_hot = (route_rank[:, :, None] == jnp.arange(CAP, dtype=jnp.int32)[None, None, :]).astype(
        jnp.float32
    )
    codes = gate_codes.astype(jnp.float32)
    gate_weight = codes / jnp.sum(codes, axis=-1, keepdims=True)
    selector = jnp.einsum("tke,tkc->ect", onehot.astype(jnp.float32), slot_hot)
    weighted_sel = jnp.einsum("tke,tkc,tk->ect", onehot.astype(jnp.float32), slot_hot, gate_weight)
    col_start = dev_id * feat_width
    split = group_count * dev_count // EXPERTS
    share = lax.psum_scatter(
        partial_value.astype(jnp.bfloat16), "dev", scatter_dimension=1, tiled=True
    ).astype(jnp.float32)
    mixed = resid.astype(jnp.float32) + share
    total_sq = lax.psum(jnp.sum(mixed * mixed, axis=1), "dev")
    gain_mine = lax.dynamic_slice_in_dim(norm_gain, col_start, feat_width).astype(jnp.float32)
    normed = (
        mixed * lax.rsqrt(total_sq / model_width + 1e-05)[:, None] * gain_mine[None, :]
    ).astype(jnp.bfloat16)
    slot_rows = jnp.einsum(
        "ect,tf->ecf", selector.astype(jnp.bfloat16), normed, preferred_element_type=jnp.float32
    ).astype(jnp.bfloat16)
    send_rows = jnp.broadcast_to(slot_rows[:, None], (EXPERTS, split, CAP, feat_width)).reshape(
        group_count * dev_count, CAP, feat_width
    )
    received = lax.all_to_all(send_rows, ("grp", "dev"), split_axis=0, concat_axis=0, tiled=True)
    slot_count = received.shape[1]
    rows = (
        received.reshape(group_count, dev_count, slot_count, feat_width)
        .transpose(0, 2, 1, 3)
        .reshape(group_count * slot_count, model_width)
    )
    outputs = expert_ffn(rows, w_gate, w_up, w_down)
    back = (
        outputs.reshape(group_count, slot_count, dev_count, feat_width)
        .transpose(0, 2, 1, 3)
        .reshape(group_count * dev_count, slot_count, feat_width)
    )
    returned = lax.all_to_all(
        back.astype(jnp.bfloat16), ("grp", "dev"), split_axis=0, concat_axis=0, tiled=True
    ).astype(back.dtype)
    expert_sums = jnp.sum(returned.reshape(EXPERTS, split, CAP, feat_width), axis=1)
    moe = jnp.einsum("ect,ecf->tf", weighted_sel, expert_sums, precision=lax.Precision.HIGHEST)
    layer_out = (mixed + moe).astype(jnp.bfloat16)
    return (new_cache_k, new_cache_v, layer_out)


MESH = pl.DeviceIdType.MESH
BF = jnp.bfloat16
F32 = jnp.float32
SLOTS = 17
NT = 512


def ask(cond):
    return cond.astype(jnp.int32)


def layer_kernel(
    ck_hbm, cv_hbm, source, lengths, query, new_key, new_value, resid, ow_hbm, gain,
    wg_hbm, wu_hbm, wd_hbm, ids_ref, codes_ref,
    nk_hbm, nv_hbm, out_ref,
    ck, cv, rk, rv, sk, sv, nk, nv,
    mask_ref, cs, cr, ss, sr, attn_ref, po, pr, mixed_ref,
    d1s, d1r, d2s, xr, acc_g, acc_u, hid, oacc, r1s, r1r, r2s, r2r, r3s, r3r, wt_ref,
    wbuf, wsem, csem, osem,
    ms_send, ms_recv, a_send, a_recv, st_send, st_recv, p_send, p_recv,
    e1_send, e1_recv, e2_send, e2_recv, e3_send, e3_recv,
    b1_send, b1_recv, b2_send, b2_recv, b3_send, b3_recv,
):
    G, N = 4, 8
    g = lax.axis_index("grp")
    d = lax.axis_index("dev")
    z, c = d // 2, d % 2
    feat = resid.shape[1]
    width = feat * N
    hidden = wbuf.shape[2]
    block_len = ck.shape[2]

    def grp_peer(i):
        return (lax.rem(g + i, G), d)

    def dev_peer(i):
        return (g, lax.rem(d + i, N))

    def z_peer(i):
        return (g, lax.rem(z + i, 4) * 2 + c)

    sibling = (g, z * 2 + 1 - c)

    def chunk_dev(k):
        return lax.rem(z + k % 4, 4) * 2 + (c if k < 4 else 1 - c)

    def remote(src, dst, send, recv, to):
        return pltpu.make_async_remote_copy(
            src_ref=src, dst_ref=dst, send_sem=send, recv_sem=recv, device_id=to, device_id_type=MESH
        )

    own_k = pltpu.make_async_copy(ck_hbm, ck, csem.at[0])
    own_v = pltpu.make_async_copy(cv_hbm, cv, csem.at[1])
    own_k.start()
    own_v.start()

    def load_rows(hbm, rows, slot, sem):
        return pltpu.make_async_copy(
            hbm.at[pl.ds(pl.multiple_of(rows, feat), feat)], wbuf.at[slot], wsem.at[sem]
        )

    out_loads = [
        pltpu.make_async_copy(ow_hbm.at[:, pl.ds(b * hidden, hidden)], wbuf.at[b], wsem.at[b])
        for b in range(3)
    ]
    gate_loads = [load_rows(wg_hbm, chunk_dev(k) * feat, 3 + k, 3 + k) for k in range(8)]
    up_slot = [11, 12, 13, 14, 15, 16, 0, 1]
    up_loads = [load_rows(wu_hbm, chunk_dev(k) * feat, up_slot[k], 11 + k) for k in range(8)]
    down_slot = [2, 3, 11, 4, 12, 5, 13, 6, 14]
    down_rows = [(0, feat), (feat, feat), (2 * feat, hidden - 2 * feat)]
    down_loads = []
    for n in range(9):
        col, (start, size) = n // 3, down_rows[n % 3]
        down_loads.append(
            pltpu.make_async_copy(
                wd_hbm.at[pl.ds(start, size), pl.ds(col * hidden, hidden)],
                wbuf.at[down_slot[n], pl.ds(0, size)],
                wsem.at[19 + n],
            )
        )

    barrier = pltpu.get_barrier_semaphore()
    for i in range(1, G):
        pl.semaphore_signal(barrier, inc=1, device_id=grp_peer(i), device_id_type=MESH)
    for i in range(1, N):
        pl.semaphore_signal(barrier, inc=1, device_id=dev_peer(i), device_id_type=MESH)
    for load in out_loads:
        load.start()
    for k in range(8):
        gate_loads[k].start()
        if k < 6:
            up_loads[k].start()

    zero = jnp.int32(0)
    own_k.wait()
    own_v.wait()
    for i in range(1, G):
        q = lax.rem(g + i, G)
        first, second, seen = zero, zero, zero
        for s in range(16):
            v = source[q * 16 + s] - g * 16
            mine = ask(v >= 0) * ask(v < 16)
            first = first + mine * ask(seen == 0) * v
            second = second + mine * ask(seen == 1) * v
            seen = seen + mine
        at = 2 * (i - 1)
        sk[at] = ck[first]
        sk[at + 1] = ck[second]
        sv[at] = cv[first]
        sv[at + 1] = cv[second]

    pl.semaphore_wait(barrier, G - 1 + N - 1)

    moves = []
    for i in range(1, G):
        part = pl.ds(2 * (i - 1), 2)
        for t, (src, dst) in enumerate(((sk, rk), (sv, rv))):
            move = remote(
                src.at[part], dst.at[part], ms_send.at[t, i], ms_recv.at[t, i], grp_peer(i)
            )
            move.start()
            moves.append(move)

    lane = lax.broadcasted_iota(jnp.int32, (96, 16 * block_len), 1)
    row = lax.broadcasted_iota(jnp.int32, (96, 16 * block_len), 0)
    limit = jnp.zeros((96, 16 * block_len), jnp.int32)
    for s in range(16):
        limit = jnp.where(lane // block_len == s, lengths[s], limit)
    inside = (d * block_len + lane % block_len <= limit) & (lane // block_len == row % 16)
    mask_ref[...] = jnp.where(inside, 1.0, 0.0)

    expert_of = lax.broadcasted_iota(jnp.int32, (16, 64), 1) // 8
    slot_of = lax.broadcasted_iota(jnp.int32, (16, 64), 1) % 8
    codes = codes_ref[...].astype(F32)
    total_code = codes[:, 0:1] + codes[:, 1:2]
    hot0 = jnp.where(ids_ref[:, 0:1] == expert_of, 1.0, 0.0)
    hot1 = jnp.where(ids_ref[:, 1:2] == expert_of, 1.0, 0.0)
    hot = hot0 + hot1
    t_row = lax.broadcasted_iota(jnp.int32, (16, 16), 0)
    t_col = lax.broadcasted_iota(jnp.int32, (16, 16), 1)
    lower = jnp.where(t_col < t_row, 1.0, 0.0).astype(BF)
    rank = jnp.dot(lower, hot.astype(BF), preferred_element_type=F32)
    placed = jnp.where(rank == slot_of.astype(F32), 1.0, 0.0)
    wt_ref[0] = hot * placed
    wt_ref[1] = (hot0 * (codes[:, 0:1] / total_code) + hot1 * (codes[:, 1:2] / total_code)) * placed

    for move in moves:
        move.wait_recv()

    counts = [zero] * G
    p_iota = lax.broadcasted_iota(jnp.int32, (8, block_len, 128), 1)
    for s in range(16):
        origin = source[g * 16 + s] // 16
        off = lax.rem(g - origin + G, G)
        at = zero
        for i in range(1, G):
            here = ask(off == i)
            at = at + here * (2 * (i - 1) + counts[i])
            counts[i] = counts[i] + here
        at = jnp.minimum(at, 5)
        stays = jnp.full((8, block_len, 128), off, jnp.int32) == 0
        hit = p_iota == lengths[s] - d * block_len
        for own, got, new, dst in ((ck, rk, new_key, nk), (cv, rv, new_value, nv)):
            kept = jnp.where(stays, own[s].astype(F32), got[at].astype(F32))
            fresh = jnp.broadcast_to(new[s].astype(F32)[:, None, :], (8, block_len, 128))
            dst[s] = jnp.where(hit, fresh, kept).astype(BF)

    put_k = pltpu.make_async_copy(nk, nk_hbm, osem.at[0])
    put_v = pltpu.make_async_copy(nv, nv_hbm, osem.at[1])
    put_k.start()
    put_v.start()

    stat_lane = lax.broadcasted_iota(jnp.int32, (96, 128), 1)

    def attend(i):
        h = lax.rem(d + i, N)
        rows = [
            query[:, pl.ds(pl.multiple_of((h * 6 + j) * 128, 128), 128)] for j in range(6)
        ]
        q_h = jnp.concatenate(rows, axis=0)
        k_h = nk[:, pl.ds(h, 1)].reshape(16 * block_len, 128)
        v_h = nv[:, pl.ds(h, 1)].reshape(16 * block_len, 128)
        valid = mask_ref[...] > 0.5
        scores = lax.dot_general(q_h, k_h, (((1,), (1,)), ((), ())), preferred_element_type=F32)
        scores = jnp.where(valid, scores / 128**0.5, F32(-1e30))
        peak = jnp.max(scores, axis=1, keepdims=True)
        weights = jnp.where(valid, jnp.exp(scores - peak), 0.0)
        total = jnp.sum(weights, axis=1, keepdims=True)
        cs[i] = jnp.dot(weights.astype(BF), v_h, preferred_element_type=F32).astype(BF)
        stat = jnp.where(stat_lane == 0, peak, jnp.where(stat_lane == 1, total, 0.0))
        stat = jnp.concatenate([stat, jnp.zeros((32, 128), F32)], axis=0)
        ss[i] = jnp.transpose(stat)[0:8]

    def send_state(i):
        return (
            remote(cs.at[i], cr.at[i], a_send.at[i], a_recv.at[i], dev_peer(i)),
            remote(ss.at[i], sr.at[i], st_send.at[i], st_recv.at[i], dev_peer(i)),
        )

    def attend_step(i, carry):
        attend(i)
        for copy in send_state(i):
            copy.start()
        return carry

    lax.fori_loop(1, N, attend_step, 0)
    attend(0)
    cr[0] = cs[0]
    sr[0] = ss[0]
    for i in range(1, N):
        for copy in send_state(i):
            copy.wait_recv()

    peaks = jnp.concatenate([sr[i, 0:1] for i in range(N)], axis=0)
    totals = jnp.concatenate([sr[i, 1:2] for i in range(N)], axis=0)
    scale = jnp.exp(peaks - jnp.max(peaks, axis=0, keepdims=True))
    norm = jnp.sum(scale * totals, axis=0, keepdims=True)
    norm = jnp.where(lax.broadcasted_iota(jnp.int32, (1, 128), 1) < 96, norm, 1.0)
    factor = jnp.concatenate([scale / norm, jnp.zeros((120, 128), F32)], axis=0)
    factor = jnp.transpose(factor)
    context = jnp.zeros((96, 128), F32)
    for i in range(N):
        context = context + cr[i].astype(F32) * factor[0:96, i : i + 1]
    for j in range(6):
        attn_ref[:, j * 128 : (j + 1) * 128] = context[j * 16 : (j + 1) * 16].astype(BF)

    for b in range(3):
        out_loads[b].wait()

        def project(n, carry, b=b):
            cols = pl.ds(pl.multiple_of(n * NT, NT), NT)
            value = jnp.dot(attn_ref[...], wbuf[b, :, cols], preferred_element_type=F32)
            po[:, pl.ds(pl.multiple_of(b * hidden + n * NT, NT), NT)] = value.astype(BF)
            return carry

        lax.fori_loop(0, hidden // NT, project, 0)
    up_loads[6].start()
    up_loads[7].start()
    down_loads[0].start()

    def feat_cols(j):
        return pl.ds(pl.multiple_of(j * feat, feat), feat)

    def send_partial(i):
        return remote(
            po.at[:, feat_cols(lax.rem(d + i, N))], pr.at[i], p_send.at[i], p_recv.at[i], dev_peer(i)
        )

    for i in range(1, N):
        send_partial(i).start()
    mixed = resid[...].astype(F32) + po[:, feat_cols(d)].astype(F32)
    for i in range(1, N):
        send_partial(i).wait_recv()
        mixed = mixed + pr[i].astype(F32)
    mixed_ref[...] = mixed

    square = jnp.sum(mixed * mixed, axis=1, keepdims=True)
    high = square.astype(BF).astype(F32)
    tail_lane = lax.broadcasted_iota(jnp.int32, (16, 128), 1)
    tail = jnp.where(tail_lane == 0, high, jnp.where(tail_lane == 1, square - high, 0.0))
    scaled = mixed * gain[:, feat_cols(d)].astype(F32)
    ext = jnp.concatenate([scaled, tail], axis=1).astype(BF)
    routed = lax.dot_general(
        wt_ref[0].astype(BF), ext, (((0,), (0,)), ((), ())), preferred_element_type=F32
    ).astype(BF)
    for q in range(G):
        d1s[q] = routed[q * 16 : (q + 1) * 16]

    def send_routed(i):
        return remote(
            d1s.at[lax.rem(g + i, G)], d1r.at[g], e1_send.at[i], e1_recv.at[i], grp_peer(i)
        )

    for i in range(1, G):
        send_routed(i).start()
    d1r[g] = d1s[g]
    for i in range(1, G):
        send_routed(i).wait_recv()
    arrived = [d1r[q].astype(F32) for q in range(G)]
    for e in range(2):
        d2s[e] = jnp.concatenate([a[e * 8 : (e + 1) * 8] for a in arrived], axis=0).astype(BF)

    def send_rows(i):
        return remote(
            d2s.at[lax.rem(z + i, 4) // 2], xr.at[4 - i], e2_send.at[4 - i], e2_recv.at[4 - i], z_peer(i)
        )

    def send_core(k):
        return remote(xr.at[k], xr.at[4 + k], e3_send.at[k], e3_recv.at[k], sibling)

    for i in (2, 1, 3):
        send_rows(i).start()
    xr[0] = d2s[z // 2]
    send_core(0).start()

    def feed(k):
        gate_loads[k].wait()
        up_loads[k].wait()

        def tile(n, carry):
            cols = pl.ds(pl.multiple_of(n * NT, NT), NT)
            rows = xr[k, :, 0:feat]
            more_g = jnp.dot(rows, wbuf[3 + k, :, cols], preferred_element_type=F32)
            more_u = jnp.dot(rows, wbuf[up_slot[k], :, cols], preferred_element_type=F32)
            if k == 0:
                acc_g[:, cols] = more_g
                acc_u[:, cols] = more_u
            else:
                acc_g[:, cols] += more_g
                acc_u[:, cols] += more_u
            return carry

        lax.fori_loop(0, hidden // NT, tile, 0)
        if k < 4:
            down_loads[2 * k + 1].start()
            down_loads[2 * k + 2].start()

    feed(0)
    for k in (1, 3, 2):
        send_rows(4 - k).wait_recv()
        send_core(k).start()
    for k in (1, 2, 3):
        feed(k)
    for k in range(4):
        send_core(k).wait_recv()
    for k in range(4, 8):
        feed(k)

    squares = jnp.zeros((32, 1), F32)
    for k in range(8):
        squares = squares + jnp.sum(xr[k, :, feat:].astype(F32), axis=1, keepdims=True)
    inv = lax.rsqrt(squares / width + 1e-05)
    gate_val = acc_g[...] * inv
    hid[...] = (gate_val / (1.0 + jnp.exp(-gate_val)) * (acc_u[...] * inv)).astype(BF)

    for n in range(9):
        down_loads[n].wait()
        col, (start, size) = n // 3, down_rows[n % 3]

        def tile(m, carry, n=n, col=col, start=start, size=size):
            cols = pl.ds(pl.multiple_of(m * NT, NT), NT)
            to = pl.ds(pl.multiple_of(col * hidden + m * NT, NT), NT)
            more = jnp.dot(
                hid[:, start : start + size],
                wbuf[down_slot[n], 0:size, cols],
                preferred_element_type=F32,
            )
            if n % 3 == 0:
                oacc[:, to] = more
            else:
                oacc[:, to] += more
            return carry

        lax.fori_loop(0, hidden // NT, tile, 0)

    def back_core(k):
        return remote(r1s.at[k], r1r.at[k], b1_send.at[k], b1_recv.at[k], sibling)

    def back_rows(k):
        return remote(r2s.at[k], r2r.at[k], b2_send.at[k], b2_recv.at[k], z_peer(k))

    def back_group(i):
        return remote(
            r3s.at[lax.rem(g + i, G)], r3r.at[g], b3_send.at[i], b3_recv.at[i], grp_peer(i)
        )

    for k in (2, 1, 3, 0):
        r1s[k] = oacc[:, feat_cols(chunk_dev(4 + k))].astype(BF)
        back_core(k).start()
    for k in (2, 1, 3, 0):
        back_core(k).wait_recv()
        value = oacc[:, feat_cols(chunk_dev(k))] + r1r[k].astype(F32)
        if k:
            r2s[k] = value.astype(BF)
            back_rows(k).start()
    even_share = 1.0 - (z // 2).astype(F32)
    even = value * even_share
    odd = value * (1.0 - even_share)
    for k in range(1, 4):
        back_rows(k).wait_recv()
        share = 1.0 - (lax.rem(z - k + 4, 4) // 2).astype(F32)
        value = r2r[k].astype(F32)
        even = even + value * share
        odd = odd + value * (1.0 - share)
    for q in range(G):
        r3s[q] = jnp.concatenate([even[q * 8 : q * 8 + 8], odd[q * 8 : q * 8 + 8]], axis=0).astype(BF)
    for i in range(1, G):
        back_group(i).start()
    r3r[g] = r3s[g]
    for i in range(1, G):
        back_group(i).wait_recv()
    rows = jnp.concatenate([r3r[q] for q in range(G)], axis=0)
    wt_high = wt_ref[1].astype(BF)
    wt_low = (wt_ref[1] - wt_high.astype(F32)).astype(BF)
    moe = jnp.dot(wt_high, rows, preferred_element_type=F32) + jnp.dot(
        wt_low, rows, preferred_element_type=F32
    )
    out_ref[...] = (mixed_ref[...] + moe).astype(BF)

    put_k.wait()
    put_v.wait()
    for move in moves:
        move.wait_send()
    for i in range(1, N):
        for copy in send_state(i):
            copy.wait_send()
        send_partial(i).wait_send()
    for i in range(1, G):
        send_routed(i).wait_send()
        send_rows(i).wait_send()
        back_rows(i).wait_send()
        back_group(i).wait_send()
    for k in range(4):
        send_core(k).wait_send()
        back_core(k).wait_send()


def fused_layer(
    cache_k, cache_v, source, lengths, query, new_key, new_value, resid, out_weight, norm_gain,
    w_gate, w_up, w_down, expert_ids, gate_codes,
):
    feat = resid.shape[1]
    width = query.shape[1]
    hidden = w_gate.shape[1]
    ext = feat + 128
    block = cache_k.shape[1:]
    vm = pl.BlockSpec(memory_space=pltpu.VMEM)
    sm = pl.BlockSpec(memory_space=pltpu.SMEM)
    far = pl.BlockSpec(memory_space=pl.ANY)
    dma = pltpu.SemaphoreType.DMA

    def buf(shape, kind=BF):
        return pltpu.VMEM(shape, kind)

    scratch = [
        buf((16, *block)), buf((16, *block)), buf((6, *block)), buf((6, *block)),
        buf((6, *block)), buf((6, *block)), buf((16, *block)), buf((16, *block)),
        buf((96, 16 * block[1]), F32), buf((8, 96, 128)), buf((8, 96, 128)),
        buf((8, 8, 128), F32), buf((8, 8, 128), F32), buf((16, feat)), buf((16, width)),
        buf((8, 16, feat)), buf((16, feat), F32),
        buf((4, 16, ext)), buf((4, 16, ext)), buf((2, 32, ext)), buf((8, 32, ext)),
        buf((32, hidden), F32), buf((32, hidden), F32), buf((32, hidden)), buf((32, width), F32),
        buf((4, 32, feat)), buf((4, 32, feat)), buf((4, 32, feat)), buf((4, 32, feat)),
        buf((4, 16, feat)), buf((4, 16, feat)), buf((2, 16, 64), F32),
        buf((SLOTS, feat, hidden)), dma((28,)), dma((2,)), dma((2,)),
        dma((2, 4)), dma((2, 4)), dma((8,)), dma((8,)), dma((8,)), dma((8,)), dma((8,)), dma((8,)),
        dma((4,)), dma((4,)), dma((4,)), dma((4,)), dma((4,)), dma((4,)),
        dma((4,)), dma((4,)), dma((4,)), dma((4,)), dma((4,)), dma((4,)),
    ]
    return pl.pallas_call(
        layer_kernel,
        out_shape=(
            jax.ShapeDtypeStruct(cache_k.shape, BF),
            jax.ShapeDtypeStruct(cache_v.shape, BF),
            jax.ShapeDtypeStruct(resid.shape, BF),
        ),
        in_specs=[far, far, sm, sm, vm, vm, vm, vm, far, vm, far, far, far, vm, vm],
        out_specs=(far, far, vm),
        scratch_shapes=scratch,
        compiler_params=pltpu.CompilerParams(
            collective_id=0, has_side_effects=True, vmem_limit_bytes=(64 << 20) - (256 << 10)
        ),
        cost_estimate=pl.CostEstimate(
            flops=2 * 32 * 3 * width * hidden, bytes_accessed=6 * width * hidden, transcendentals=0
        ),
    )(
        cache_k, cache_v, source, lengths, query, new_key, new_value, resid, out_weight,
        norm_gain.reshape(1, -1), w_gate, w_up, w_down, expert_ids, gate_codes,
    )


def device_program(*args):
    cache_k, query, resid, w_gate = args[0], args[4], args[7], args[10]
    fits = (
        lax.axis_size("grp") == 4
        and lax.axis_size("dev") == cache_k.shape[1]
        and resid.shape[1] * lax.axis_size("dev") == query.shape[1]
        and w_gate.shape[1] * 3 == query.shape[1]
        and cache_k.shape[0] == 16
    )
    return fused_layer(*args) if fits else on_device(*args)


def solution(mesh):
    in_specs = (
        P("grp", None, "dev", None),
        P("grp", None, "dev", None),
        P(),
        P("grp"),
        P("grp", None),
        P("grp", None, None),
        P("grp", None, None),
        P("grp", "dev"),
        P("dev", None),
        P(),
        P(None, ("grp", "dev")),
        P(None, ("grp", "dev")),
        P(("grp", "dev"), None),
        P("grp", None),
        P("grp", None),
    )
    out_specs = (P("grp", None, "dev", None), P("grp", None, "dev", None), P("grp", "dev"))
    return jax.shard_map(
        device_program, mesh=mesh, in_specs=in_specs, out_specs=out_specs, check_vma=False
    )
```

```python
import jax
import jax.numpy as jnp
from jax import lax
from jax.experimental import pallas as pl
from jax.experimental.pallas import tpu as pltpu
from jax.sharding import PartitionSpec as P

EXPERTS = 8
TOP = 2
MOVE = 2
CAP = 8


def joined(array, axis, combine):
    everything = jax.tree.map(
        lambda part, kind: lax.all_gather(part.astype(kind), axis),
        array,
        (jnp.bfloat16, jnp.bfloat16, jnp.bfloat16),
    )

    def take(k):
        return jax.tree.map(lambda part, own: part[k].astype(own.dtype), everything, array)

    return lax.fori_loop(
        1, lax.axis_size(axis), lambda k, so_far: combine(so_far, take(k)), take(0)
    )


def expert_ffn(rows, w_gate, w_up, w_down):
    gate_val = jnp.dot(rows, w_gate, preferred_element_type=jnp.float32)
    up_val = jnp.dot(rows, w_up, preferred_element_type=jnp.float32)
    hidden = (jax.nn.silu(gate_val) * up_val).astype(jnp.bfloat16)
    return jnp.dot(hidden, w_down, preferred_element_type=jnp.float32)


def merge_states(earlier, later):
    top = jnp.maximum(earlier[0], later[0])
    first_scale = jnp.exp(earlier[0] - top)
    second_scale = jnp.exp(later[0] - top)
    totals = earlier[1] * first_scale + later[1] * second_scale
    context = earlier[2] * first_scale[..., None] + later[2] * second_scale[..., None]
    return (top, totals, context)


def on_device(
    cache_k,
    cache_v,
    source,
    lengths,
    query,
    new_key,
    new_value,
    resid,
    out_weight,
    norm_gain,
    w_gate,
    w_up,
    w_down,
    expert_ids,
    gate_codes,
):
    group_count = lax.axis_size("grp")
    dev_count = lax.axis_size("dev")
    group_id = lax.axis_index("grp")
    dev_id = lax.axis_index("dev")
    per_group, kv_heads, block_len, head_dim = cache_k.shape
    all_slots = source.shape[0]
    model_width = resid.shape[1] * dev_count
    feat_width = resid.shape[1]
    slot_range = jnp.arange(all_slots, dtype=jnp.int32)
    inverse = jnp.sum(
        jnp.where(source[:, None] == slot_range[None, :], slot_range[:, None], 0), axis=0
    )
    old_group = slot_range // per_group
    dest_group = inverse // per_group
    leaving = dest_group != old_group
    same_route = (old_group[:, None] == old_group[None, :]) & (
        dest_group[:, None] == dest_group[None, :]
    )
    earlier_movers = same_route & leaving[None, :] & (slot_range[None, :] < slot_range[:, None])
    mover_rank = jnp.sum(earlier_movers.astype(jnp.int32), axis=1)
    first_slot = group_id * per_group
    my_leaving = lax.dynamic_slice_in_dim(leaving, first_slot, per_group)
    my_dest = lax.dynamic_slice_in_dim(dest_group, first_slot, per_group)
    my_rank = lax.dynamic_slice_in_dim(mover_rank, first_slot, per_group)
    buffer_range = jnp.arange(group_count * MOVE, dtype=jnp.int32)
    local_range = jnp.arange(per_group, dtype=jnp.int32)
    match = (
        my_leaving[None, :]
        & (my_dest[None, :] == (buffer_range // MOVE)[:, None])
        & (my_rank[None, :] == (buffer_range % MOVE)[:, None])
    )
    picked = jnp.sum(jnp.where(match, local_range[None, :], 0), axis=1)
    filled = jnp.any(match, axis=1)[:, None, None, None]
    zero_block = jnp.zeros((), jnp.bfloat16)
    send_k = jnp.where(filled, jnp.take(cache_k, picked, axis=0), zero_block)
    send_v = jnp.where(filled, jnp.take(cache_v, picked, axis=0), zero_block)
    recv_k, recv_v = (
        lax.all_to_all(send_k, "grp", split_axis=0, concat_axis=0, tiled=True),
        lax.all_to_all(send_v, "grp", split_axis=0, concat_axis=0, tiled=True),
    )
    my_source = lax.dynamic_slice_in_dim(source, first_slot, per_group)
    source_group = my_source // per_group
    arrival = per_group + source_group * MOVE + jnp.take(mover_rank, my_source)
    where_from = jnp.where(source_group == group_id, my_source - first_slot, arrival)
    moved_k = jnp.take(jnp.concatenate([cache_k, recv_k], axis=0), where_from, axis=0)
    moved_v = jnp.take(jnp.concatenate([cache_v, recv_v], axis=0), where_from, axis=0)
    positions = dev_id * block_len + jnp.arange(block_len, dtype=jnp.int32)
    hit = (positions[None, :] == lengths[:, None])[:, None, :, None]
    new_cache_k = jnp.where(hit, new_key[:, :, None, :], moved_k)
    new_cache_v = jnp.where(hit, new_value[:, :, None, :], moved_v)
    share_heads = query.shape[1] // (kv_heads * head_dim)
    grouped = query.reshape(per_group, kv_heads, share_heads, head_dim)
    scores = (
        jnp.einsum("rkgh,rkph->rkgp", grouped, new_cache_k, preferred_element_type=jnp.float32)
        / head_dim**0.5
    )
    valid = (positions[None, :] <= lengths[:, None])[:, None, None, :]
    scores = jnp.where(valid, scores, jnp.float32(-1e30))
    local_peak = jnp.max(scores, axis=-1)
    values_wide = new_cache_v.astype(jnp.float32)
    weights = jnp.where(valid, jnp.exp(scores - local_peak[..., None]), jnp.float32(0.0))
    local_total = jnp.sum(weights, axis=-1)
    local_context = jnp.einsum(
        "rkgp,rkph->rkgh", weights, values_wide, precision=lax.Precision.HIGHEST
    )
    peak, totals, context = joined((local_peak, local_total, local_context), "dev", merge_states)
    attn = (context / totals[..., None]).reshape(per_group, -1).astype(jnp.bfloat16)
    row_count = out_weight.shape[0]
    attn_mine = lax.dynamic_slice_in_dim(attn, dev_id * row_count, row_count, 1)
    partial_value = jnp.dot(attn_mine, out_weight, preferred_element_type=jnp.float32)
    expert_range = jnp.arange(EXPERTS, dtype=jnp.int32)
    onehot = expert_ids[:, :, None] == expert_range[None, None, :]
    flat_hot = onehot.reshape(per_group * TOP, EXPERTS).astype(jnp.int32)
    before = jnp.cumsum(flat_hot, axis=0) - flat_hot
    route_rank = jnp.sum(before * flat_hot, axis=1).reshape(per_group, TOP)
    slot_hot = (route_rank[:, :, None] == jnp.arange(CAP, dtype=jnp.int32)[None, None, :]).astype(
        jnp.float32
    )
    codes = gate_codes.astype(jnp.float32)
    gate_weight = codes / jnp.sum(codes, axis=-1, keepdims=True)
    selector = jnp.einsum("tke,tkc->ect", onehot.astype(jnp.float32), slot_hot)
    weighted_sel = jnp.einsum("tke,tkc,tk->ect", onehot.astype(jnp.float32), slot_hot, gate_weight)
    col_start = dev_id * feat_width
    split = group_count * dev_count // EXPERTS
    share = lax.psum_scatter(
        partial_value.astype(jnp.bfloat16), "dev", scatter_dimension=1, tiled=True
    ).astype(jnp.float32)
    mixed = resid.astype(jnp.float32) + share
    total_sq = lax.psum(jnp.sum(mixed * mixed, axis=1), "dev")
    gain_mine = lax.dynamic_slice_in_dim(norm_gain, col_start, feat_width).astype(jnp.float32)
    normed = (
        mixed * lax.rsqrt(total_sq / model_width + 1e-05)[:, None] * gain_mine[None, :]
    ).astype(jnp.bfloat16)
    slot_rows = jnp.einsum(
        "ect,tf->ecf", selector.astype(jnp.bfloat16), normed, preferred_element_type=jnp.float32
    ).astype(jnp.bfloat16)
    send_rows = jnp.broadcast_to(slot_rows[:, None], (EXPERTS, split, CAP, feat_width)).reshape(
        group_count * dev_count, CAP, feat_width
    )
    received = lax.all_to_all(send_rows, ("grp", "dev"), split_axis=0, concat_axis=0, tiled=True)
    slot_count = received.shape[1]
    rows = (
        received.reshape(group_count, dev_count, slot_count, feat_width)
        .transpose(0, 2, 1, 3)
        .reshape(group_count * slot_count, model_width)
    )
    outputs = expert_ffn(rows, w_gate, w_up, w_down)
    back = (
        outputs.reshape(group_count, slot_count, dev_count, feat_width)
        .transpose(0, 2, 1, 3)
        .reshape(group_count * dev_count, slot_count, feat_width)
    )
    returned = lax.all_to_all(
        back.astype(jnp.bfloat16), ("grp", "dev"), split_axis=0, concat_axis=0, tiled=True
    ).astype(back.dtype)
    expert_sums = jnp.sum(returned.reshape(EXPERTS, split, CAP, feat_width), axis=1)
    moe = jnp.einsum("ect,ecf->tf", weighted_sel, expert_sums, precision=lax.Precision.HIGHEST)
    layer_out = (mixed + moe).astype(jnp.bfloat16)
    return (new_cache_k, new_cache_v, layer_out)


MESH = pl.DeviceIdType.MESH
BF = jnp.bfloat16
F32 = jnp.float32
SLOTS = 16


def ask(cond):
    return cond.astype(jnp.int32)


def layer_kernel(
    ck_hbm, cv_hbm, source, lengths, query, new_key, new_value, resid, ow_hbm, gain,
    wg_hbm, wu_hbm, wd_hbm, ids_ref, codes_ref,
    nk_hbm, nv_hbm, out_ref,
    ck, cv, rk, rv, sk, sv, nk, nv,
    mask_ref, ws, cs, cr, ss, sr, attn_ref, po, pr, mixed_ref,
    d1s, d1r, d2s, xr, acc_g, acc_u, hid, oacc, r1s, r1r, r2s, r2r, r3s, r3r, wt_ref,
    wbuf, wsem, csem, osem,
    ms_send, ms_recv, a_send, a_recv, st_send, st_recv, p_send, p_recv,
    e1_send, e1_recv, e2_send, e2_recv, e3_send, e3_recv,
    b1_send, b1_recv, b2_send, b2_recv, b3_send, b3_recv,
):
    G, N = 4, 8
    g = lax.axis_index("grp")
    d = lax.axis_index("dev")
    z, c = d // 2, d % 2
    feat = resid.shape[1]
    width = feat * N
    hidden = wbuf.shape[2]
    block_len = ck.shape[2]

    def grp_peer(i):
        return (lax.rem(g + i, G), d)

    def dev_peer(i):
        return (g, lax.rem(d + i, N))

    def z_peer(i):
        return (g, lax.rem(z + i, 4) * 2 + c)

    sibling = (g, z * 2 + 1 - c)

    def chunk_dev(k):
        other = k // 4
        return lax.rem(z + k % 4, 4) * 2 + c + other * (1 - 2 * c)

    def remote(src, dst, send, recv, to):
        return pltpu.make_async_remote_copy(
            src_ref=src, dst_ref=dst, send_sem=send, recv_sem=recv, device_id=to, device_id_type=MESH
        )

    own_k = pltpu.make_async_copy(ck_hbm, ck, csem.at[0])
    own_v = pltpu.make_async_copy(cv_hbm, cv, csem.at[1])
    own_k.start()
    own_v.start()

    pair = 2 * feat

    def pair_cols(k):
        return pl.ds(pl.multiple_of(lax.rem(z + k, 4) * pair, pair), pair)

    def gate_slot(k):
        return 4 + k

    def up_slot(k):
        return lax.rem(12 + k, SLOTS)

    def down_slot(n):
        return (4 + n // 2) * (1 - n % 2) + lax.rem(12 + n // 2, SLOTS) * (n % 2)

    def load_rows(hbm, k, slot, sem):
        rows = pl.ds(pl.multiple_of(chunk_dev(k) * feat, feat), feat)
        return pltpu.make_async_copy(hbm.at[rows], wbuf.at[slot], wsem.at[sem])

    def load_gate(k):
        return load_rows(wg_hbm, k, gate_slot(k), 4 + k)

    def load_up(k):
        return load_rows(wu_hbm, k, up_slot(k), 12 + k)

    def load_out(b):
                return pltpu.make_async_copy(
            ow_hbm.at[:, pair_cols(b + 1)], wbuf.at[b, :, pl.ds(0, pair)], wsem.at[b]
        )

    down_rows = [(0, feat), (feat, feat), (2 * feat, hidden - 2 * feat)]

    def load_down(t, r):
        start, size = down_rows[r]
        n = 3 * t + r
        return pltpu.make_async_copy(
            wd_hbm.at[pl.ds(start, size), pair_cols(t + 1)],
            wbuf.at[down_slot(n), pl.ds(0, size), pl.ds(0, pair)],
            wsem.at[20 + n],
        )

    barrier = pltpu.get_barrier_semaphore()
    for i in range(1, G):
        pl.semaphore_signal(barrier, inc=1, device_id=grp_peer(i), device_id_type=MESH)
    for i in range(1, N):
        pl.semaphore_signal(barrier, inc=1, device_id=dev_peer(i), device_id_type=MESH)
    for b in range(4):
        load_out(b).start()
    for k in range(8):
        load_gate(k).start()
        if k < 4:
            load_up(k).start()

    zero = jnp.int32(0)
    own_k.wait()
    own_v.wait()
    for i in range(1, G):
        q = lax.rem(g + i, G)
        first, second, seen = zero, zero, zero
        for s in range(16):
            v = source[q * 16 + s] - g * 16
            mine = ask(v >= 0) * ask(v < 16)
            first = first + mine * ask(seen == 0) * v
            second = second + mine * ask(seen == 1) * v
            seen = seen + mine
        at = 2 * (i - 1)
        sk[at] = ck[first]
        sk[at + 1] = ck[second]
        sv[at] = cv[first]
        sv[at + 1] = cv[second]

    pl.semaphore_wait(barrier, G - 1 + N - 1)

    moves = []
    for t, (src, dst) in enumerate(((sk, rk), (sv, rv))):
        for i in range(1, G):
            part = pl.ds(2 * (i - 1), 2)
            move = remote(
                src.at[part], dst.at[part], ms_send.at[t, i], ms_recv.at[t, i], grp_peer(i)
            )
            move.start()
            moves.append(move)

    lane = lax.broadcasted_iota(jnp.int32, (96, 16 * block_len), 1)
    row = lax.broadcasted_iota(jnp.int32, (96, 16 * block_len), 0)
    limit = jnp.zeros((96, 16 * block_len), jnp.int32)
    for s in range(16):
        limit = jnp.where(lane // block_len == s, lengths[s], limit)
    inside = (d * block_len + lane % block_len <= limit) & (lane // block_len == row % 16)
    mask_ref[...] = jnp.where(inside, 1.0, 0.0)

    expert_of = lax.broadcasted_iota(jnp.int32, (64, 16), 0) // 8
    slot_of = lax.broadcasted_iota(jnp.int32, (64, 16), 0) % 8
    codes = codes_ref[...].astype(F32)
    total_code = codes[0:1] + codes[1:2]
    hot0 = jnp.where(ids_ref[0:1, :] == expert_of, 1.0, 0.0)
    hot1 = jnp.where(ids_ref[1:2, :] == expert_of, 1.0, 0.0)
    hot = hot0 + hot1
    t_row = lax.broadcasted_iota(jnp.int32, (16, 16), 0)
    t_col = lax.broadcasted_iota(jnp.int32, (16, 16), 1)
    upper = jnp.where(t_row < t_col, 1.0, 0.0).astype(BF)
    rank = jnp.dot(hot.astype(BF), upper, preferred_element_type=F32)
    placed = jnp.where(rank == slot_of.astype(F32), 1.0, 0.0)
    wt_ref[0] = hot * placed
    wt_ref[1] = (hot0 * (codes[0:1] / total_code) + hot1 * (codes[1:2] / total_code)) * placed

    counts = [zero] * G
    p_iota = lax.broadcasted_iota(jnp.int32, (8, block_len, 128), 1)
    places = []
    for s in range(16):
        origin = source[g * 16 + s] // 16
        off = lax.rem(g - origin + G, G)
        at = zero
        for i in range(1, G):
            here = ask(off == i)
            at = at + here * (2 * (i - 1) + counts[i])
            counts[i] = counts[i] + here
        places.append((off, jnp.minimum(at, 5)))

    def build(own, got, new, dst):
        for s, (off, at) in enumerate(places):
            stays = jnp.full((8, block_len, 128), off, jnp.int32) == 0
            hit = p_iota == lengths[s] - d * block_len
            kept = jnp.where(stays, own[s].astype(F32), got[at].astype(F32))
            fresh = jnp.broadcast_to(new[s].astype(F32)[:, None, :], (8, block_len, 128))
            dst[s] = jnp.where(hit, fresh, kept).astype(BF)

    for move in moves[: G - 1]:
        move.wait_recv()
    build(ck, rk, new_key, nk)
    put_k = pltpu.make_async_copy(nk, nk_hbm, osem.at[0])
    put_v = pltpu.make_async_copy(nv, nv_hbm, osem.at[1])
    put_k.start()

    stat_lane = lax.broadcasted_iota(jnp.int32, (96, 128), 1)

    def score(i):
        h = lax.rem(d + i, N)
        rows = [
            query[:, pl.ds(pl.multiple_of((h * 6 + j) * 128, 128), 128)] for j in range(6)
        ]
        q_h = jnp.concatenate(rows, axis=0)
        k_h = nk[:, pl.ds(h, 1)].reshape(16 * block_len, 128)
        valid = mask_ref[...] > 0.5
        scores = lax.dot_general(q_h, k_h, (((1,), (1,)), ((), ())), preferred_element_type=F32)
        scores = jnp.where(valid, scores / 128**0.5, F32(-1e30))
        peak = jnp.max(scores, axis=1, keepdims=True)
        weights = jnp.where(valid, jnp.exp(scores - peak), 0.0)
        total = jnp.sum(weights, axis=1, keepdims=True)
        ws[i] = weights.astype(BF)
        stat = jnp.where(stat_lane == 0, peak, jnp.where(stat_lane == 1, total, 0.0))
        stat = jnp.concatenate([stat, jnp.zeros((32, 128), F32)], axis=0)
        ss[i] = jnp.transpose(stat)[0:8]

    def score_step(m, carry):
        score(2 * m)
        score(2 * m + 1)
        return carry

    lax.fori_loop(0, N // 2, score_step, 0)

    def attend(i):
        v_h = nv[:, pl.ds(lax.rem(d + i, N), 1)].reshape(16 * block_len, 128)
        cs[i] = jnp.dot(ws[i], v_h, preferred_element_type=F32).astype(BF)

    for move in moves[G - 1 :]:
        move.wait_recv()
    build(cv, rv, new_value, nv)
    put_v.start()

    def send_state(i):
        return (
            remote(cs.at[i], cr.at[i], a_send.at[i], a_recv.at[i], dev_peer(i)),
            remote(ss.at[i], sr.at[i], st_send.at[i], st_recv.at[i], dev_peer(i)),
        )

    def attend_step(i, carry):
        attend(i)
        for copy in send_state(i):
            copy.start()
        return carry

    for i in range(1, N):
        attend_step(i, 0)
    attend(0)
    cr[0] = cs[0]
    sr[0] = ss[0]
    for i in range(1, N):
        for copy in send_state(i):
            copy.wait_recv()

    peaks = jnp.concatenate([sr[i, 0:1] for i in range(N)], axis=0)
    totals = jnp.concatenate([sr[i, 1:2] for i in range(N)], axis=0)
    scale = jnp.exp(peaks - jnp.max(peaks, axis=0, keepdims=True))
    norm = jnp.sum(scale * totals, axis=0, keepdims=True)
    norm = jnp.where(lax.broadcasted_iota(jnp.int32, (1, 128), 1) < 96, norm, 1.0)
    factor = jnp.concatenate([scale / norm, jnp.zeros((120, 128), F32)], axis=0)
    factor = jnp.transpose(factor)
    context = jnp.zeros((96, 128), F32)
    for i in range(N):
        context = context + cr[i].astype(F32) * factor[0:96, i : i + 1]
    for j in range(6):
        attn_ref[:, j * 128 : (j + 1) * 128] = context[j * 16 : (j + 1) * 16].astype(BF)

    def feat_cols(j):
        return pl.ds(pl.multiple_of(j * feat, feat), feat)

    def send_partial(k, core):
        at = 2 * k + core
        return remote(
            po.at[k, :, feat_cols(core)],
            pr.at[2 * k + c],
            p_send.at[at],
            p_recv.at[2 * k + c],
            (g, lax.rem(z + k, 4) * 2 + core),
        )

    def core_partial():
        return remote(po.at[0, :, feat_cols(1 - c)], pr.at[0], p_send.at[0], p_recv.at[0], sibling)

    for b in range(4):
        load_out(b).wait()
        k = (b + 1) % 4
        value = jnp.dot(
            attn_ref[...], wbuf[b, :, 0:pair], preferred_element_type=F32
        )
        po[k] = value.astype(BF)
        if k:
            send_partial(k, 0).start()
            send_partial(k, 1).start()
        else:
            core_partial().start()
    for k in range(4, 8):
        load_up(k).start()

    mixed = resid[...].astype(F32) + po[0, :, feat_cols(c)].astype(F32)
    core_partial().wait_recv()
    mixed = mixed + pr[0].astype(F32)
    for at in range(2, N):
        remote(
            po.at[0, :, feat_cols(0)], pr.at[at], p_send.at[1], p_recv.at[at], sibling
        ).wait_recv()
        mixed = mixed + pr[at].astype(F32)
    mixed_ref[...] = mixed

    square = jnp.sum(mixed * mixed, axis=1, keepdims=True)
    high = square.astype(BF).astype(F32)
    tail_lane = lax.broadcasted_iota(jnp.int32, (16, 128), 1)
    tail = jnp.where(tail_lane == 0, high, jnp.where(tail_lane == 1, square - high, 0.0))
    scaled = mixed * gain[:, feat_cols(d)].astype(F32)
    ext = jnp.concatenate([scaled, tail], axis=1).astype(BF)
    routed = lax.dot_general(
        wt_ref[0].astype(BF), ext, (((1,), (0,)), ((), ())), preferred_element_type=F32
    ).astype(BF)
    for q in range(G):
        d1s[q] = routed[q * 16 : (q + 1) * 16]

    def send_routed(i):
        return remote(
            d1s.at[lax.rem(g + i, G)], d1r.at[g], e1_send.at[i], e1_recv.at[i], grp_peer(i)
        )

    for i in range(1, G):
        send_routed(i).start()
    d1r[g] = d1s[g]
    for i in range(1, G):
        send_routed(i).wait_recv()
    arrived = [d1r[q].astype(F32) for q in range(G)]
    for e in range(2):
        d2s[e] = jnp.concatenate([a[e * 8 : (e + 1) * 8] for a in arrived], axis=0).astype(BF)

    def send_rows(i):
        return remote(
            d2s.at[lax.rem(z + i, 4) // 2], xr.at[4 - i], e2_send.at[4 - i], e2_recv.at[4 - i], z_peer(i)
        )

    def send_core(k):
        return remote(xr.at[k], xr.at[4 + k], e3_send.at[k], e3_recv.at[k], sibling)

    for i in (2, 1, 3):
        send_rows(i).start()
    xr[0] = d2s[z // 2]
    send_core(0).start()

    def feed(k):
        load_gate(k).wait()
        load_up(k).wait()
        rows = xr[k, :, 0:feat]
        value_g = jnp.dot(rows, wbuf[gate_slot(k)], preferred_element_type=F32)
        value_u = jnp.dot(rows, wbuf[up_slot(k)], preferred_element_type=F32)
        if isinstance(k, int):
            acc_g[...] = value_g
            acc_u[...] = value_u
        else:
            acc_g[...] += value_g
            acc_u[...] += value_u

    def feed_step(k, carry):
        feed(k)
        return carry

    def start_downs(k):
        for n in (2 * k, 2 * k + 1):
            load_down(n // 3, n % 3).start()

    feed(0)
    start_downs(0)
    for k in (1, 3, 2):
        send_rows(4 - k).wait_recv()
        send_core(k).start()
    lax.fori_loop(1, 4, feed_step, 0)
    for k in range(1, 4):
        start_downs(k)
    for k in range(4):
        send_core(k).wait_recv()
    lax.fori_loop(4, 6, feed_step, 0)
    for k in range(4, 6):
        start_downs(k)
    lax.fori_loop(6, 8, feed_step, 0)

    squares = jnp.zeros((32, 1), F32)
    for k in range(8):
        squares = squares + jnp.sum(xr[k, :, feat:].astype(F32), axis=1, keepdims=True)
    inv = lax.rsqrt(squares / width + 1e-05)
    gate_val = acc_g[...] * inv
    hid[...] = (gate_val / (1.0 + jnp.exp(-gate_val)) * (acc_u[...] * inv)).astype(BF)

    def back_core(k):
        return remote(r1s.at[k], r1r.at[k], b1_send.at[k], b1_recv.at[k], sibling)

    def back_rows(k):
        return remote(r2s.at[k], r2r.at[k], b2_send.at[k], b2_recv.at[k], z_peer(k + 1))

    def back_group(i):
        return remote(
            r3s.at[lax.rem(g + i, G)], r3r.at[g], b3_send.at[i], b3_recv.at[i], grp_peer(i)
        )

    def expand(t):
        value = jnp.zeros((32, pair), F32)
        for r, (start, size) in enumerate(down_rows):
            load_down(t, r).wait()
            value = value + jnp.dot(
                hid[:, start : start + size],
                wbuf[down_slot(3 * t + r), 0:size, 0:pair],
                preferred_element_type=F32,
            )
        oacc[t] = value
        r1s[t] = oacc[t, :, feat_cols(1 - c)].astype(BF)
        back_core(t).start()

    def joined_share(t):
        back_core(t).wait_recv()
        return oacc[t, :, feat_cols(c)] + r1r[t].astype(F32)

    def expand_step(t, carry):
        expand(t)
        r2s[t - 1] = joined_share(t - 1).astype(BF)
        back_rows(t - 1).start()
        return carry

    expand(0)
    lax.fori_loop(1, 4, expand_step, 0)
    value = joined_share(3)
    even_share = 1.0 - (z // 2).astype(F32)
    even = value * even_share
    odd = value * (1.0 - even_share)
    for t in range(3):
        back_rows(t).wait_recv()
        share = 1.0 - (lax.rem(z - t + 3, 4) // 2).astype(F32)
        value = r2r[t].astype(F32)
        even = even + value * share
        odd = odd + value * (1.0 - share)
    for q in range(G):
        r3s[q] = jnp.concatenate([even[q * 8 : q * 8 + 8], odd[q * 8 : q * 8 + 8]], axis=0).astype(BF)
    for i in range(1, G):
        back_group(i).start()
    r3r[g] = r3s[g]
    for i in range(1, G):
        back_group(i).wait_recv()
    rows = jnp.concatenate([r3r[q] for q in range(G)], axis=0)
    wt_high = wt_ref[1].astype(BF)
    wt_low = (wt_ref[1] - wt_high.astype(F32)).astype(BF)
    moe = sum(
        lax.dot_general(part, rows, (((0,), (0,)), ((), ())), preferred_element_type=F32)
        for part in (wt_high, wt_low)
    )
    out_ref[...] = (mixed_ref[...] + moe).astype(BF)

    put_k.wait()
    put_v.wait()
    for move in moves:
        move.wait_send()
    for i in range(1, N):
        for copy in send_state(i):
            copy.wait_send()
    core_partial().wait_send()
    for k in range(1, 4):
        send_partial(k, 0).wait_send()
        send_partial(k, 1).wait_send()
    for i in range(1, G):
        send_routed(i).wait_send()
        send_rows(i).wait_send()
        back_rows(i - 1).wait_send()
        back_group(i).wait_send()
    for k in range(4):
        send_core(k).wait_send()
        back_core(k).wait_send()


def hand_over(k_in, v_in, out_in, k_out, v_out, out_out, sems):
    copies = [pltpu.make_async_copy(out_in, out_out, sems.at[8])]
    quarter = k_in.shape[0] // 4
    for n in range(4):
        part = pl.ds(n * quarter, quarter)
        copies.append(pltpu.make_async_copy(k_in.at[part], k_out.at[part], sems.at[2 * n]))
        copies.append(pltpu.make_async_copy(v_in.at[part], v_out.at[part], sems.at[2 * n + 1]))
    for copy in copies:
        copy.start()
    for copy in copies:
        copy.wait()


def fused_layer(
    cache_k, cache_v, source, lengths, query, new_key, new_value, resid, out_weight, norm_gain,
    w_gate, w_up, w_down, expert_ids, gate_codes,
):
    feat = resid.shape[1]
    width = query.shape[1]
    hidden = w_gate.shape[1]
    ext = feat + 128
    block = cache_k.shape[1:]
    vm = pl.BlockSpec(memory_space=pltpu.VMEM)
    sm = pl.BlockSpec(memory_space=pltpu.SMEM)
    far = pl.BlockSpec(memory_space=pl.ANY)
    dma = pltpu.SemaphoreType.DMA

    def buf(shape, kind=BF):
        return pltpu.VMEM(shape, kind)

    scratch = [
        buf((16, *block)), buf((16, *block)), buf((6, *block)), buf((6, *block)),
        buf((6, *block)), buf((6, *block)), buf((16, *block)), buf((16, *block)),
        buf((96, 16 * block[1]), F32), buf((8, 96, 16 * block[1])), buf((8, 96, 128)), buf((8, 96, 128)),
        buf((8, 8, 128), F32), buf((8, 8, 128), F32), buf((16, feat)), buf((4, 16, 2 * feat)),
        buf((8, 16, feat)), buf((16, feat), F32),
        buf((4, 16, ext)), buf((4, 16, ext)), buf((2, 32, ext)), buf((8, 32, ext)),
        buf((32, hidden), F32), buf((32, hidden), F32), buf((32, hidden)), buf((4, 32, 2 * feat), F32),
        buf((4, 32, feat)), buf((4, 32, feat)), buf((4, 32, feat)), buf((4, 32, feat)),
        buf((4, 16, feat)), buf((4, 16, feat)), buf((2, 64, 16), F32),
        buf((SLOTS, feat, hidden)), dma((32,)), dma((2,)), dma((2,)),
        dma((2, 4)), dma((2, 4)), dma((8,)), dma((8,)), dma((8,)), dma((8,)), dma((8,)), dma((8,)),
        dma((4,)), dma((4,)), dma((4,)), dma((4,)), dma((4,)), dma((4,)),
        dma((4,)), dma((4,)), dma((4,)), dma((4,)), dma((4,)), dma((4,)),
    ]
    results = pl.pallas_call(
        layer_kernel,
        out_shape=(
            jax.ShapeDtypeStruct(cache_k.shape, BF),
            jax.ShapeDtypeStruct(cache_v.shape, BF),
            jax.ShapeDtypeStruct(resid.shape, BF),
        ),
        in_specs=[far, far, sm, sm, vm, vm, vm, vm, far, vm, far, far, far, vm, vm],
        out_specs=(far, far, vm),
        scratch_shapes=scratch,
        compiler_params=pltpu.CompilerParams(
            collective_id=0, has_side_effects=True, vmem_limit_bytes=(64 << 20) - (256 << 10)
        ),
        cost_estimate=pl.CostEstimate(
            flops=2 * 32 * 3 * width * hidden, bytes_accessed=6 * width * hidden, transcendentals=0
        ),
    )(
        cache_k, cache_v, source, lengths, query, new_key, new_value, resid, out_weight,
        norm_gain.reshape(1, -1), w_gate, w_up, w_down, expert_ids.T, gate_codes.T,
    )
    return pl.pallas_call(
        hand_over,
        out_shape=tuple(jax.ShapeDtypeStruct(r.shape, r.dtype) for r in results),
        in_specs=[far] * 3,
        out_specs=(far,) * 3,
        scratch_shapes=[dma((9,))],
        cost_estimate=pl.CostEstimate(flops=0, bytes_accessed=8 << 20, transcendentals=0),
    )(*results)


def device_program(*args):
    cache_k, query, resid, w_gate = args[0], args[4], args[7], args[10]
    fits = (
        lax.axis_size("grp") == 4
        and lax.axis_size("dev") == cache_k.shape[1]
        and resid.shape[1] * lax.axis_size("dev") == query.shape[1]
        and w_gate.shape[1] * 3 == query.shape[1]
        and cache_k.shape[0] == 16
    )
    return fused_layer(*args) if fits else on_device(*args)


def solution(mesh):
    in_specs = (
        P("grp", None, "dev", None),
        P("grp", None, "dev", None),
        P(),
        P("grp"),
        P("grp", None),
        P("grp", None, None),
        P("grp", None, None),
        P("grp", "dev"),
        P("dev", None),
        P(),
        P(None, ("grp", "dev")),
        P(None, ("grp", "dev")),
        P(("grp", "dev"), None),
        P("grp", None),
        P("grp", None),
    )
    out_specs = (P("grp", None, "dev", None), P("grp", None, "dev", None), P("grp", "dev"))
    return jax.shard_map(
        device_program, mesh=mesh, in_specs=in_specs, out_specs=out_specs, check_vma=False
    )
```

```python
import jax
import jax.numpy as jnp
from jax import lax
from jax.experimental import pallas as pl
from jax.experimental.pallas import tpu as pltpu
from jax.sharding import PartitionSpec as P

EXPERTS = 8
TOP = 2
MOVE = 2
CAP = 8


def joined(array, axis, combine):
    everything = jax.tree.map(
        lambda part, kind: lax.all_gather(part.astype(kind), axis),
        array,
        (jnp.bfloat16, jnp.bfloat16, jnp.bfloat16),
    )

    def take(k):
        return jax.tree.map(lambda part, own: part[k].astype(own.dtype), everything, array)

    return lax.fori_loop(
        1, lax.axis_size(axis), lambda k, so_far: combine(so_far, take(k)), take(0)
    )


def expert_ffn(rows, w_gate, w_up, w_down):
    gate_val = jnp.dot(rows, w_gate, preferred_element_type=jnp.float32)
    up_val = jnp.dot(rows, w_up, preferred_element_type=jnp.float32)
    hidden = (jax.nn.silu(gate_val) * up_val).astype(jnp.bfloat16)
    return jnp.dot(hidden, w_down, preferred_element_type=jnp.float32)


def merge_states(earlier, later):
    top = jnp.maximum(earlier[0], later[0])
    first_scale = jnp.exp(earlier[0] - top)
    second_scale = jnp.exp(later[0] - top)
    totals = earlier[1] * first_scale + later[1] * second_scale
    context = earlier[2] * first_scale[..., None] + later[2] * second_scale[..., None]
    return (top, totals, context)


def on_device(
    cache_k,
    cache_v,
    source,
    lengths,
    query,
    new_key,
    new_value,
    resid,
    out_weight,
    norm_gain,
    w_gate,
    w_up,
    w_down,
    expert_ids,
    gate_codes,
):
    group_count = lax.axis_size("grp")
    dev_count = lax.axis_size("dev")
    group_id = lax.axis_index("grp")
    dev_id = lax.axis_index("dev")
    per_group, kv_heads, block_len, head_dim = cache_k.shape
    all_slots = source.shape[0]
    model_width = resid.shape[1] * dev_count
    feat_width = resid.shape[1]
    slot_range = jnp.arange(all_slots, dtype=jnp.int32)
    inverse = jnp.sum(
        jnp.where(source[:, None] == slot_range[None, :], slot_range[:, None], 0), axis=0
    )
    old_group = slot_range // per_group
    dest_group = inverse // per_group
    leaving = dest_group != old_group
    same_route = (old_group[:, None] == old_group[None, :]) & (
        dest_group[:, None] == dest_group[None, :]
    )
    earlier_movers = same_route & leaving[None, :] & (slot_range[None, :] < slot_range[:, None])
    mover_rank = jnp.sum(earlier_movers.astype(jnp.int32), axis=1)
    first_slot = group_id * per_group
    my_leaving = lax.dynamic_slice_in_dim(leaving, first_slot, per_group)
    my_dest = lax.dynamic_slice_in_dim(dest_group, first_slot, per_group)
    my_rank = lax.dynamic_slice_in_dim(mover_rank, first_slot, per_group)
    buffer_range = jnp.arange(group_count * MOVE, dtype=jnp.int32)
    local_range = jnp.arange(per_group, dtype=jnp.int32)
    match = (
        my_leaving[None, :]
        & (my_dest[None, :] == (buffer_range // MOVE)[:, None])
        & (my_rank[None, :] == (buffer_range % MOVE)[:, None])
    )
    picked = jnp.sum(jnp.where(match, local_range[None, :], 0), axis=1)
    filled = jnp.any(match, axis=1)[:, None, None, None]
    zero_block = jnp.zeros((), jnp.bfloat16)
    send_k = jnp.where(filled, jnp.take(cache_k, picked, axis=0), zero_block)
    send_v = jnp.where(filled, jnp.take(cache_v, picked, axis=0), zero_block)
    recv_k, recv_v = (
        lax.all_to_all(send_k, "grp", split_axis=0, concat_axis=0, tiled=True),
        lax.all_to_all(send_v, "grp", split_axis=0, concat_axis=0, tiled=True),
    )
    my_source = lax.dynamic_slice_in_dim(source, first_slot, per_group)
    source_group = my_source // per_group
    arrival = per_group + source_group * MOVE + jnp.take(mover_rank, my_source)
    where_from = jnp.where(source_group == group_id, my_source - first_slot, arrival)
    moved_k = jnp.take(jnp.concatenate([cache_k, recv_k], axis=0), where_from, axis=0)
    moved_v = jnp.take(jnp.concatenate([cache_v, recv_v], axis=0), where_from, axis=0)
    positions = dev_id * block_len + jnp.arange(block_len, dtype=jnp.int32)
    hit = (positions[None, :] == lengths[:, None])[:, None, :, None]
    new_cache_k = jnp.where(hit, new_key[:, :, None, :], moved_k)
    new_cache_v = jnp.where(hit, new_value[:, :, None, :], moved_v)
    share_heads = query.shape[1] // (kv_heads * head_dim)
    grouped = query.reshape(per_group, kv_heads, share_heads, head_dim)
    scores = (
        jnp.einsum("rkgh,rkph->rkgp", grouped, new_cache_k, preferred_element_type=jnp.float32)
        / head_dim**0.5
    )
    valid = (positions[None, :] <= lengths[:, None])[:, None, None, :]
    scores = jnp.where(valid, scores, jnp.float32(-1e30))
    local_peak = jnp.max(scores, axis=-1)
    values_wide = new_cache_v.astype(jnp.float32)
    weights = jnp.where(valid, jnp.exp(scores - local_peak[..., None]), jnp.float32(0.0))
    local_total = jnp.sum(weights, axis=-1)
    local_context = jnp.einsum(
        "rkgp,rkph->rkgh", weights, values_wide, precision=lax.Precision.HIGHEST
    )
    peak, totals, context = joined((local_peak, local_total, local_context), "dev", merge_states)
    attn = (context / totals[..., None]).reshape(per_group, -1).astype(jnp.bfloat16)
    row_count = out_weight.shape[0]
    attn_mine = lax.dynamic_slice_in_dim(attn, dev_id * row_count, row_count, 1)
    partial_value = jnp.dot(attn_mine, out_weight, preferred_element_type=jnp.float32)
    expert_range = jnp.arange(EXPERTS, dtype=jnp.int32)
    onehot = expert_ids[:, :, None] == expert_range[None, None, :]
    flat_hot = onehot.reshape(per_group * TOP, EXPERTS).astype(jnp.int32)
    before = jnp.cumsum(flat_hot, axis=0) - flat_hot
    route_rank = jnp.sum(before * flat_hot, axis=1).reshape(per_group, TOP)
    slot_hot = (route_rank[:, :, None] == jnp.arange(CAP, dtype=jnp.int32)[None, None, :]).astype(
        jnp.float32
    )
    codes = gate_codes.astype(jnp.float32)
    gate_weight = codes / jnp.sum(codes, axis=-1, keepdims=True)
    selector = jnp.einsum("tke,tkc->ect", onehot.astype(jnp.float32), slot_hot)
    weighted_sel = jnp.einsum("tke,tkc,tk->ect", onehot.astype(jnp.float32), slot_hot, gate_weight)
    col_start = dev_id * feat_width
    split = group_count * dev_count // EXPERTS
    share = lax.psum_scatter(
        partial_value.astype(jnp.bfloat16), "dev", scatter_dimension=1, tiled=True
    ).astype(jnp.float32)
    mixed = resid.astype(jnp.float32) + share
    total_sq = lax.psum(jnp.sum(mixed * mixed, axis=1), "dev")
    gain_mine = lax.dynamic_slice_in_dim(norm_gain, col_start, feat_width).astype(jnp.float32)
    normed = (
        mixed * lax.rsqrt(total_sq / model_width + 1e-05)[:, None] * gain_mine[None, :]
    ).astype(jnp.bfloat16)
    slot_rows = jnp.einsum(
        "ect,tf->ecf", selector.astype(jnp.bfloat16), normed, preferred_element_type=jnp.float32
    ).astype(jnp.bfloat16)
    send_rows = jnp.broadcast_to(slot_rows[:, None], (EXPERTS, split, CAP, feat_width)).reshape(
        group_count * dev_count, CAP, feat_width
    )
    received = lax.all_to_all(send_rows, ("grp", "dev"), split_axis=0, concat_axis=0, tiled=True)
    slot_count = received.shape[1]
    rows = (
        received.reshape(group_count, dev_count, slot_count, feat_width)
        .transpose(0, 2, 1, 3)
        .reshape(group_count * slot_count, model_width)
    )
    outputs = expert_ffn(rows, w_gate, w_up, w_down)
    back = (
        outputs.reshape(group_count, slot_count, dev_count, feat_width)
        .transpose(0, 2, 1, 3)
        .reshape(group_count * dev_count, slot_count, feat_width)
    )
    returned = lax.all_to_all(
        back.astype(jnp.bfloat16), ("grp", "dev"), split_axis=0, concat_axis=0, tiled=True
    ).astype(back.dtype)
    expert_sums = jnp.sum(returned.reshape(EXPERTS, split, CAP, feat_width), axis=1)
    moe = jnp.einsum("ect,ecf->tf", weighted_sel, expert_sums, precision=lax.Precision.HIGHEST)
    layer_out = (mixed + moe).astype(jnp.bfloat16)
    return (new_cache_k, new_cache_v, layer_out)


MESH = pl.DeviceIdType.MESH
BF = jnp.bfloat16
F32 = jnp.float32
SLOTS = 16


def ask(cond):
    return cond.astype(jnp.int32)


def layer_kernel(
    ck_hbm, cv_hbm, source, lengths, query, new_key, new_value, resid, ow_hbm, gain,
    wg_hbm, wu_hbm, wd_hbm, ids_ref, codes_ref,
    nk_hbm, nv_hbm, out_ref,
    ck, cv, rk, rv, sk, sv, nk, nv,
    mask_ref, ws, cs, cr, ss, sr, attn_ref, po, pr, mixed_ref,
    d1s, d1r, d2s, xr, acc_g, acc_u, hid, oacc, r1s, r1r, r2s, r2r, r3s, r3r, wt_ref,
    wbuf, wsem, csem, osem,
    ms_send, ms_recv, a_send, a_recv, st_send, st_recv, p_send, p_recv,
    e1_send, e1_recv, e2_send, e2_recv, e3_send, e3_recv,
    b1_send, b1_recv, b2_send, b2_recv, b3_send, b3_recv,
):
    G, N = 4, 8
    g = lax.axis_index("grp")
    d = lax.axis_index("dev")
    z, c = d // 2, d % 2
    feat = resid.shape[1]
    width = feat * N
    hidden = wbuf.shape[2]
    block_len = ck.shape[2]

    def grp_peer(i):
        return (lax.rem(g + i, G), d)

    def dev_peer(i):
        return (g, lax.rem(d + i, N))

    def z_peer(i):
        return (g, lax.rem(z + i, 4) * 2 + c)

    sibling = (g, z * 2 + 1 - c)

    def chunk_dev(k):
        other = k // 4
        return lax.rem(z + k % 4, 4) * 2 + c + other * (1 - 2 * c)

    def remote(src, dst, send, recv, to):
        return pltpu.make_async_remote_copy(
            src_ref=src, dst_ref=dst, send_sem=send, recv_sem=recv, device_id=to, device_id_type=MESH
        )

    own_k = pltpu.make_async_copy(ck_hbm, ck, csem.at[0])
    own_v = pltpu.make_async_copy(cv_hbm, cv, csem.at[1])
    own_k.start()
    own_v.start()

    pair = 2 * feat

    def pair_cols(k):
        return pl.ds(pl.multiple_of(lax.rem(z + k, 4) * pair, pair), pair)

    def gate_slot(k):
        return 4 + k

    def up_slot(k):
        return lax.rem(12 + k, SLOTS)

    def down_slot(n):
        return (4 + n // 2) * (1 - n % 2) + lax.rem(12 + n // 2, SLOTS) * (n % 2)

    def load_rows(hbm, k, slot, sem):
        rows = pl.ds(pl.multiple_of(chunk_dev(k) * feat, feat), feat)
        return pltpu.make_async_copy(hbm.at[rows], wbuf.at[slot], wsem.at[sem])

    order = (0, 4, 1, 3, 2, 5, 7, 6)

    def load_gate(p, k):
        return load_rows(wg_hbm, k, gate_slot(p), 4 + p)

    def load_up(p, k):
        return load_rows(wu_hbm, k, up_slot(p), 12 + p)

    def load_out(b):
                return pltpu.make_async_copy(
            ow_hbm.at[:, pair_cols(b + 1)], wbuf.at[b, :, pl.ds(0, pair)], wsem.at[b]
        )

    down_rows = [(0, feat), (feat, feat), (2 * feat, hidden - 2 * feat)]

    def load_down(t, r):
        start, size = down_rows[r]
        n = 3 * t + r
        return pltpu.make_async_copy(
            wd_hbm.at[pl.ds(start, size), pair_cols(t + 1)],
            wbuf.at[down_slot(n), pl.ds(0, size), pl.ds(0, pair)],
            wsem.at[20 + n],
        )

    barrier = pltpu.get_barrier_semaphore()
    for i in range(1, G):
        pl.semaphore_signal(barrier, inc=1, device_id=grp_peer(i), device_id_type=MESH)
    for i in range(1, N):
        pl.semaphore_signal(barrier, inc=1, device_id=dev_peer(i), device_id_type=MESH)
    for b in range(4):
        load_out(b).start()
    for p, k in enumerate(order):
        load_gate(p, k).start()
        if p < 4:
            load_up(p, k).start()

    zero = jnp.int32(0)
    own_k.wait()
    own_v.wait()
    for i in range(1, G):
        q = lax.rem(g + i, G)
        first, second, seen = zero, zero, zero
        for s in range(16):
            v = source[q * 16 + s] - g * 16
            mine = ask(v >= 0) * ask(v < 16)
            first = first + mine * ask(seen == 0) * v
            second = second + mine * ask(seen == 1) * v
            seen = seen + mine
        at = 2 * (i - 1)
        sk[at] = ck[first]
        sk[at + 1] = ck[second]
        sv[at] = cv[first]
        sv[at + 1] = cv[second]

    pl.semaphore_wait(barrier, G - 1 + N - 1)

    moves = []
    for t, (src, dst) in enumerate(((sk, rk), (sv, rv))):
        for i in range(1, G):
            part = pl.ds(2 * (i - 1), 2)
            move = remote(
                src.at[part], dst.at[part], ms_send.at[t, i], ms_recv.at[t, i], grp_peer(i)
            )
            move.start()
            moves.append(move)

    lane = lax.broadcasted_iota(jnp.int32, (96, 16 * block_len), 1)
    row = lax.broadcasted_iota(jnp.int32, (96, 16 * block_len), 0)
    limit = jnp.zeros((96, 16 * block_len), jnp.int32)
    for s in range(16):
        limit = jnp.where(lane // block_len == s, lengths[s], limit)
    inside = (d * block_len + lane % block_len <= limit) & (lane // block_len == row % 16)
    mask_ref[...] = jnp.where(inside, 1.0, 0.0)

    expert_of = lax.broadcasted_iota(jnp.int32, (64, 16), 0) // 8
    slot_of = lax.broadcasted_iota(jnp.int32, (64, 16), 0) % 8
    codes = codes_ref[...].astype(F32)
    total_code = codes[0:1] + codes[1:2]
    hot0 = jnp.where(ids_ref[0:1, :] == expert_of, 1.0, 0.0)
    hot1 = jnp.where(ids_ref[1:2, :] == expert_of, 1.0, 0.0)
    hot = hot0 + hot1
    t_row = lax.broadcasted_iota(jnp.int32, (16, 16), 0)
    t_col = lax.broadcasted_iota(jnp.int32, (16, 16), 1)
    upper = jnp.where(t_row < t_col, 1.0, 0.0).astype(BF)
    rank = jnp.dot(hot.astype(BF), upper, preferred_element_type=F32)
    placed = jnp.where(rank == slot_of.astype(F32), 1.0, 0.0)
    wt_ref[0] = hot * placed
    wt_ref[1] = (hot0 * (codes[0:1] / total_code) + hot1 * (codes[1:2] / total_code)) * placed

    counts = [zero] * G
    p_iota = lax.broadcasted_iota(jnp.int32, (8, block_len, 128), 1)
    places = []
    for s in range(16):
        origin = source[g * 16 + s] // 16
        off = lax.rem(g - origin + G, G)
        at = zero
        for i in range(1, G):
            here = ask(off == i)
            at = at + here * (2 * (i - 1) + counts[i])
            counts[i] = counts[i] + here
        places.append((off, jnp.minimum(at, 5)))

    def build(own, got, new, dst):
        for s, (off, at) in enumerate(places):
            stays = jnp.full((8, block_len, 128), off, jnp.int32) == 0
            hit = p_iota == lengths[s] - d * block_len
            kept = jnp.where(stays, own[s].astype(F32), got[at].astype(F32))
            fresh = jnp.broadcast_to(new[s].astype(F32)[:, None, :], (8, block_len, 128))
            dst[s] = jnp.where(hit, fresh, kept).astype(BF)

    for move in moves[: G - 1]:
        move.wait_recv()
    build(ck, rk, new_key, nk)
    put_k = pltpu.make_async_copy(nk, nk_hbm, osem.at[0])
    put_v = pltpu.make_async_copy(nv, nv_hbm, osem.at[1])
    put_k.start()

    stat_lane = lax.broadcasted_iota(jnp.int32, (96, 128), 1)

    def score(i):
        h = lax.rem(d + i, N)
        rows = [
            query[:, pl.ds(pl.multiple_of((h * 6 + j) * 128, 128), 128)] for j in range(6)
        ]
        q_h = jnp.concatenate(rows, axis=0)
        k_h = nk[:, pl.ds(h, 1)].reshape(16 * block_len, 128)
        valid = mask_ref[...] > 0.5
        scores = lax.dot_general(q_h, k_h, (((1,), (1,)), ((), ())), preferred_element_type=F32)
        scores = jnp.where(valid, scores / 128**0.5, F32(-1e30))
        peak = jnp.max(scores, axis=1, keepdims=True)
        weights = jnp.where(valid, jnp.exp(scores - peak), 0.0)
        total = jnp.sum(weights, axis=1, keepdims=True)
        ws[i] = weights.astype(BF)
        stat = jnp.where(stat_lane == 0, peak, jnp.where(stat_lane == 1, total, 0.0))
        stat = jnp.concatenate([stat, jnp.zeros((32, 128), F32)], axis=0)
        ss[i] = jnp.transpose(stat)[0:8]

    def score_step(m, carry):
        score(2 * m)
        score(2 * m + 1)
        return carry

    lax.fori_loop(0, N // 2, score_step, 0)

    def attend(i):
        v_h = nv[:, pl.ds(lax.rem(d + i, N), 1)].reshape(16 * block_len, 128)
        cs[i] = jnp.dot(ws[i], v_h, preferred_element_type=F32).astype(BF)

    for move in moves[G - 1 :]:
        move.wait_recv()
    build(cv, rv, new_value, nv)
    put_v.start()

    def send_state(i):
        return (
            remote(cs.at[i], cr.at[i], a_send.at[i], a_recv.at[i], dev_peer(i)),
            remote(ss.at[i], sr.at[i], st_send.at[i], st_recv.at[i], dev_peer(i)),
        )

    def attend_step(i, carry):
        attend(i)
        for copy in send_state(i):
            copy.start()
        return carry

    for i in range(1, N):
        attend_step(i, 0)
    attend(0)
    cr[0] = cs[0]
    sr[0] = ss[0]
    for i in range(1, N):
        for copy in send_state(i):
            copy.wait_recv()

    peaks = jnp.concatenate([sr[i, 0:1] for i in range(N)], axis=0)
    totals = jnp.concatenate([sr[i, 1:2] for i in range(N)], axis=0)
    scale = jnp.exp(peaks - jnp.max(peaks, axis=0, keepdims=True))
    norm = jnp.sum(scale * totals, axis=0, keepdims=True)
    norm = jnp.where(lax.broadcasted_iota(jnp.int32, (1, 128), 1) < 96, norm, 1.0)
    factor = jnp.concatenate([scale / norm, jnp.zeros((120, 128), F32)], axis=0)
    factor = jnp.transpose(factor)
    context = jnp.zeros((96, 128), F32)
    for i in range(N):
        context = context + cr[i].astype(F32) * factor[0:96, i : i + 1]
    for j in range(6):
        attn_ref[:, j * 128 : (j + 1) * 128] = context[j * 16 : (j + 1) * 16].astype(BF)

    def feat_cols(j):
        return pl.ds(pl.multiple_of(j * feat, feat), feat)

    def send_partial(k, core):
        at = 2 * k + core
        return remote(
            po.at[k, :, feat_cols(core)],
            pr.at[2 * k + c],
            p_send.at[at],
            p_recv.at[2 * k + c],
            (g, lax.rem(z + k, 4) * 2 + core),
        )

    def core_partial():
        return remote(po.at[0, :, feat_cols(1 - c)], pr.at[0], p_send.at[0], p_recv.at[0], sibling)

    for b in range(4):
        load_out(b).wait()
        k = (b + 1) % 4
        value = jnp.dot(
            attn_ref[...], wbuf[b, :, 0:pair], preferred_element_type=F32
        )
        po[k] = value.astype(BF)
        if k:
            send_partial(k, 0).start()
            send_partial(k, 1).start()
        else:
            core_partial().start()
    for p in range(4, 8):
        load_up(p, order[p]).start()

    mixed = resid[...].astype(F32) + po[0, :, feat_cols(c)].astype(F32)
    core_partial().wait_recv()
    mixed = mixed + pr[0].astype(F32)
    for at in range(2, N):
        remote(
            po.at[0, :, feat_cols(0)], pr.at[at], p_send.at[1], p_recv.at[at], sibling
        ).wait_recv()
        mixed = mixed + pr[at].astype(F32)
    mixed_ref[...] = mixed

    square = jnp.sum(mixed * mixed, axis=1, keepdims=True)
    high = square.astype(BF).astype(F32)
    tail_lane = lax.broadcasted_iota(jnp.int32, (16, 128), 1)
    tail = jnp.where(tail_lane == 0, high, jnp.where(tail_lane == 1, square - high, 0.0))
    scaled = mixed * gain[feat_cols(d)].astype(F32).reshape(1, feat)
    ext = jnp.concatenate([scaled, tail], axis=1).astype(BF)
    routed = lax.dot_general(
        wt_ref[0].astype(BF), ext, (((1,), (0,)), ((), ())), preferred_element_type=F32
    ).astype(BF)
    for q in range(G):
        d1s[q] = routed[q * 16 : (q + 1) * 16]

    def send_routed(i):
        return remote(
            d1s.at[lax.rem(g + i, G)], d1r.at[g], e1_send.at[i], e1_recv.at[i], grp_peer(i)
        )

    for i in range(1, G):
        send_routed(i).start()
    d1r[g] = d1s[g]
    for i in range(1, G):
        send_routed(i).wait_recv()
    arrived = [d1r[q].astype(F32) for q in range(G)]
    for e in range(2):
        d2s[e] = jnp.concatenate([a[e * 8 : (e + 1) * 8] for a in arrived], axis=0).astype(BF)

    def send_rows(i):
        return remote(
            d2s.at[lax.rem(z + i, 4) // 2], xr.at[4 - i], e2_send.at[4 - i], e2_recv.at[4 - i], z_peer(i)
        )

    def send_core(k):
        return remote(xr.at[k], xr.at[4 + k], e3_send.at[k], e3_recv.at[k], sibling)

    for i in (2, 1, 3):
        send_rows(i).start()
    xr[0] = d2s[z // 2]
    send_core(0).start()

    acc_g[...] = jnp.zeros(acc_g.shape, F32)
    acc_u[...] = jnp.zeros(acc_u.shape, F32)

    def feed_two(p, first, second):
        def feed(n, carry):
            k = first + n * (second - first)
            load_gate(p + n, k).wait()
            load_up(p + n, k).wait()
            rows = xr[k, :, 0:feat]
            acc_g[...] += jnp.dot(rows, wbuf[gate_slot(p + n)], preferred_element_type=F32)
            acc_u[...] += jnp.dot(rows, wbuf[up_slot(p + n)], preferred_element_type=F32)
            return carry

        lax.fori_loop(0, 2, feed, 0)
        if p < 6:
            for n in range(2 * p, 2 * p + 4):
                load_down(n // 3, n % 3).start()

    send_core(0).wait_recv()
    feed_two(0, 0, 4)
    for k in (1, 3):
        send_rows(4 - k).wait_recv()
        send_core(k).start()
    feed_two(2, 1, 3)
    send_rows(2).wait_recv()
    send_core(2).start()
    send_core(1).wait_recv()
    feed_two(4, 2, 5)
    send_core(3).wait_recv()
    send_core(2).wait_recv()
    feed_two(6, 7, 6)

    squares = jnp.zeros((32, 1), F32)
    for k in range(8):
        squares = squares + jnp.sum(xr[k, :, feat:].astype(F32), axis=1, keepdims=True)
    inv = lax.rsqrt(squares / width + 1e-05)
    gate_val = acc_g[...] * inv
    hid[...] = (gate_val / (1.0 + jnp.exp(-gate_val)) * (acc_u[...] * inv)).astype(BF)

    def back_core(k):
        return remote(r1s.at[k], r1r.at[k], b1_send.at[k], b1_recv.at[k], sibling)

    def back_rows(k):
        return remote(r2s.at[k], r2r.at[k], b2_send.at[k], b2_recv.at[k], z_peer(k + 1))

    def back_group(i):
        return remote(
            r3s.at[lax.rem(g + i, G)], r3r.at[g], b3_send.at[i], b3_recv.at[i], grp_peer(i)
        )

    def expand(t):
        value = jnp.zeros((32, pair), F32)
        for r, (start, size) in enumerate(down_rows):
            load_down(t, r).wait()
            value = value + jnp.dot(
                hid[:, start : start + size],
                wbuf[down_slot(3 * t + r), 0:size, 0:pair],
                preferred_element_type=F32,
            )
        oacc[t] = value
        r1s[t] = oacc[t, :, feat_cols(1 - c)].astype(BF)
        back_core(t).start()

    def joined_share(t):
        back_core(t).wait_recv()
        return oacc[t, :, feat_cols(c)] + r1r[t].astype(F32)

    def expand_step(t, carry):
        expand(t)
        r2s[t - 1] = joined_share(t - 1).astype(BF)
        back_rows(t - 1).start()
        return carry

    expand(0)
    lax.fori_loop(1, 4, expand_step, 0)
    value = joined_share(3)
    even_share = 1.0 - (z // 2).astype(F32)
    even = value * even_share
    odd = value * (1.0 - even_share)
    for t in range(3):
        back_rows(t).wait_recv()
        share = 1.0 - (lax.rem(z - t + 3, 4) // 2).astype(F32)
        value = r2r[t].astype(F32)
        even = even + value * share
        odd = odd + value * (1.0 - share)
    for q in range(G):
        r3s[q] = jnp.concatenate([even[q * 8 : q * 8 + 8], odd[q * 8 : q * 8 + 8]], axis=0).astype(BF)
    for i in range(1, G):
        back_group(i).start()
    r3r[g] = r3s[g]
    for i in range(1, G):
        back_group(i).wait_recv()
    rows = jnp.concatenate([r3r[q] for q in range(G)], axis=0)
    wt_high = wt_ref[1].astype(BF)
    wt_low = (wt_ref[1] - wt_high.astype(F32)).astype(BF)
    moe = sum(
        lax.dot_general(part, rows, (((0,), (0,)), ((), ())), preferred_element_type=F32)
        for part in (wt_high, wt_low)
    )
    out_ref[...] = (mixed_ref[...] + moe).astype(BF)

    put_k.wait()
    put_v.wait()
    for move in moves:
        move.wait_send()
    for i in range(1, N):
        for copy in send_state(i):
            copy.wait_send()
    core_partial().wait_send()
    for k in range(1, 4):
        send_partial(k, 0).wait_send()
        send_partial(k, 1).wait_send()
    for i in range(1, G):
        send_routed(i).wait_send()
        send_rows(i).wait_send()
        back_rows(i - 1).wait_send()
        back_group(i).wait_send()
    for k in range(4):
        send_core(k).wait_send()
        back_core(k).wait_send()


def hand_over(k_in, v_in, out_in, k_out, v_out, out_out, k_mid, v_mid, out_mid, in_sems, out_sems):
    stages = [(out_in, out_mid, out_out)]
    quarter = k_in.shape[0] // 4
    for n in range(4):
        part = pl.ds(n * quarter, quarter)
        stages.append((k_in.at[part], k_mid.at[part], k_out.at[part]))
        stages.append((v_in.at[part], v_mid.at[part], v_out.at[part]))
    first = [
        pltpu.make_async_copy(src, mid, in_sems.at[n]) for n, (src, mid, _) in enumerate(stages)
    ]
    second = [
        pltpu.make_async_copy(mid, dst, out_sems.at[n]) for n, (_, mid, dst) in enumerate(stages)
    ]
    for copy in first:
        copy.start()
    for came, goes in zip(first, second):
        came.wait()
        goes.start()
    for copy in second:
        copy.wait()


def fused_layer(
    cache_k, cache_v, source, lengths, query, new_key, new_value, resid, out_weight, norm_gain,
    w_gate, w_up, w_down, expert_ids, gate_codes,
):
    feat = resid.shape[1]
    width = query.shape[1]
    hidden = w_gate.shape[1]
    ext = feat + 128
    block = cache_k.shape[1:]
    vm = pl.BlockSpec(memory_space=pltpu.VMEM)
    sm = pl.BlockSpec(memory_space=pltpu.SMEM)
    far = pl.BlockSpec(memory_space=pl.ANY)
    dma = pltpu.SemaphoreType.DMA

    def buf(shape, kind=BF):
        return pltpu.VMEM(shape, kind)

    scratch = [
        buf((16, *block)), buf((16, *block)), buf((6, *block)), buf((6, *block)),
        buf((6, *block)), buf((6, *block)), buf((16, *block)), buf((16, *block)),
        buf((96, 16 * block[1]), F32), buf((8, 96, 16 * block[1])), buf((8, 96, 128)), buf((8, 96, 128)),
        buf((8, 8, 128), F32), buf((8, 8, 128), F32), buf((16, feat)), buf((4, 16, 2 * feat)),
        buf((8, 16, feat)), buf((16, feat), F32),
        buf((4, 16, ext)), buf((4, 16, ext)), buf((2, 32, ext)), buf((8, 32, ext)),
        buf((32, hidden), F32), buf((32, hidden), F32), buf((32, hidden)), buf((4, 32, 2 * feat), F32),
        buf((4, 32, feat)), buf((4, 32, feat)), buf((4, 32, feat)), buf((4, 32, feat)),
        buf((4, 16, feat)), buf((4, 16, feat)), buf((2, 64, 16), F32),
        buf((SLOTS, feat, hidden)), dma((32,)), dma((2,)), dma((2,)),
        dma((2, 4)), dma((2, 4)), dma((8,)), dma((8,)), dma((8,)), dma((8,)), dma((8,)), dma((8,)),
        dma((4,)), dma((4,)), dma((4,)), dma((4,)), dma((4,)), dma((4,)),
        dma((4,)), dma((4,)), dma((4,)), dma((4,)), dma((4,)), dma((4,)),
    ]
    results = pl.pallas_call(
        layer_kernel,
        out_shape=(
            jax.ShapeDtypeStruct(cache_k.shape, BF),
            jax.ShapeDtypeStruct(cache_v.shape, BF),
            jax.ShapeDtypeStruct(resid.shape, BF),
        ),
        in_specs=[far, far, sm, sm, vm, vm, vm, vm, far, vm, far, far, far, vm, vm],
        out_specs=(far, far, vm),
        scratch_shapes=scratch,
        compiler_params=pltpu.CompilerParams(
            collective_id=0, has_side_effects=True, vmem_limit_bytes=(64 << 20) - (256 << 10)
        ),
        cost_estimate=pl.CostEstimate(
            flops=2 * 32 * 3 * width * hidden, bytes_accessed=6 * width * hidden, transcendentals=0
        ),
    )(
        cache_k, cache_v, source, lengths, query, new_key, new_value, resid, out_weight,
        norm_gain, w_gate, w_up, w_down, expert_ids.T, gate_codes.T,
    )
    return pl.pallas_call(
        hand_over,
        out_shape=tuple(jax.ShapeDtypeStruct(r.shape, r.dtype) for r in results),
        in_specs=[far] * 3,
        out_specs=(far,) * 3,
        scratch_shapes=[buf(r.shape) for r in results] + [dma((9,)), dma((9,))],
        cost_estimate=pl.CostEstimate(flops=0, bytes_accessed=8 << 20, transcendentals=0),
    )(*results)


def device_program(*args):
    cache_k, query, resid, w_gate = args[0], args[4], args[7], args[10]
    fits = (
        lax.axis_size("grp") == 4
        and lax.axis_size("dev") == cache_k.shape[1]
        and resid.shape[1] * lax.axis_size("dev") == query.shape[1]
        and w_gate.shape[1] * 3 == query.shape[1]
        and cache_k.shape[0] == 16
    )
    return fused_layer(*args) if fits else on_device(*args)


def solution(mesh):
    in_specs = (
        P("grp", None, "dev", None),
        P("grp", None, "dev", None),
        P(),
        P("grp"),
        P("grp", None),
        P("grp", None, None),
        P("grp", None, None),
        P("grp", "dev"),
        P("dev", None),
        P(),
        P(None, ("grp", "dev")),
        P(None, ("grp", "dev")),
        P(("grp", "dev"), None),
        P("grp", None),
        P("grp", None),
    )
    out_specs = (P("grp", None, "dev", None), P("grp", None, "dev", None), P("grp", "dev"))
    return jax.shard_map(
        device_program, mesh=mesh, in_specs=in_specs, out_specs=out_specs, check_vma=False
    )
```

```python
import jax
import jax.numpy as jnp
from jax import lax
from jax.experimental import pallas as pl
from jax.experimental.pallas import tpu as pltpu
from jax.sharding import PartitionSpec as P

EXPERTS = 8
TOP = 2
MOVE = 2
CAP = 8


def joined(array, axis, combine):
    everything = jax.tree.map(
        lambda part, kind: lax.all_gather(part.astype(kind), axis),
        array,
        (jnp.bfloat16, jnp.bfloat16, jnp.bfloat16),
    )

    def take(k):
        return jax.tree.map(lambda part, own: part[k].astype(own.dtype), everything, array)

    return lax.fori_loop(
        1, lax.axis_size(axis), lambda k, so_far: combine(so_far, take(k)), take(0)
    )


def expert_ffn(rows, w_gate, w_up, w_down):
    gate_val = jnp.dot(rows, w_gate, preferred_element_type=jnp.float32)
    up_val = jnp.dot(rows, w_up, preferred_element_type=jnp.float32)
    hidden = (jax.nn.silu(gate_val) * up_val).astype(jnp.bfloat16)
    return jnp.dot(hidden, w_down, preferred_element_type=jnp.float32)


def merge_states(earlier, later):
    top = jnp.maximum(earlier[0], later[0])
    first_scale = jnp.exp(earlier[0] - top)
    second_scale = jnp.exp(later[0] - top)
    totals = earlier[1] * first_scale + later[1] * second_scale
    context = earlier[2] * first_scale[..., None] + later[2] * second_scale[..., None]
    return (top, totals, context)


def on_device(
    cache_k,
    cache_v,
    source,
    lengths,
    query,
    new_key,
    new_value,
    resid,
    out_weight,
    norm_gain,
    w_gate,
    w_up,
    w_down,
    expert_ids,
    gate_codes,
):
    group_count = lax.axis_size("grp")
    dev_count = lax.axis_size("dev")
    group_id = lax.axis_index("grp")
    dev_id = lax.axis_index("dev")
    per_group, kv_heads, block_len, head_dim = cache_k.shape
    all_slots = source.shape[0]
    model_width = resid.shape[1] * dev_count
    feat_width = resid.shape[1]
    slot_range = jnp.arange(all_slots, dtype=jnp.int32)
    inverse = jnp.sum(
        jnp.where(source[:, None] == slot_range[None, :], slot_range[:, None], 0), axis=0
    )
    old_group = slot_range // per_group
    dest_group = inverse // per_group
    leaving = dest_group != old_group
    same_route = (old_group[:, None] == old_group[None, :]) & (
        dest_group[:, None] == dest_group[None, :]
    )
    earlier_movers = same_route & leaving[None, :] & (slot_range[None, :] < slot_range[:, None])
    mover_rank = jnp.sum(earlier_movers.astype(jnp.int32), axis=1)
    first_slot = group_id * per_group
    my_leaving = lax.dynamic_slice_in_dim(leaving, first_slot, per_group)
    my_dest = lax.dynamic_slice_in_dim(dest_group, first_slot, per_group)
    my_rank = lax.dynamic_slice_in_dim(mover_rank, first_slot, per_group)
    buffer_range = jnp.arange(group_count * MOVE, dtype=jnp.int32)
    local_range = jnp.arange(per_group, dtype=jnp.int32)
    match = (
        my_leaving[None, :]
        & (my_dest[None, :] == (buffer_range // MOVE)[:, None])
        & (my_rank[None, :] == (buffer_range % MOVE)[:, None])
    )
    picked = jnp.sum(jnp.where(match, local_range[None, :], 0), axis=1)
    filled = jnp.any(match, axis=1)[:, None, None, None]
    zero_block = jnp.zeros((), jnp.bfloat16)
    send_k = jnp.where(filled, jnp.take(cache_k, picked, axis=0), zero_block)
    send_v = jnp.where(filled, jnp.take(cache_v, picked, axis=0), zero_block)
    recv_k, recv_v = (
        lax.all_to_all(send_k, "grp", split_axis=0, concat_axis=0, tiled=True),
        lax.all_to_all(send_v, "grp", split_axis=0, concat_axis=0, tiled=True),
    )
    my_source = lax.dynamic_slice_in_dim(source, first_slot, per_group)
    source_group = my_source // per_group
    arrival = per_group + source_group * MOVE + jnp.take(mover_rank, my_source)
    where_from = jnp.where(source_group == group_id, my_source - first_slot, arrival)
    moved_k = jnp.take(jnp.concatenate([cache_k, recv_k], axis=0), where_from, axis=0)
    moved_v = jnp.take(jnp.concatenate([cache_v, recv_v], axis=0), where_from, axis=0)
    positions = dev_id * block_len + jnp.arange(block_len, dtype=jnp.int32)
    hit = (positions[None, :] == lengths[:, None])[:, None, :, None]
    new_cache_k = jnp.where(hit, new_key[:, :, None, :], moved_k)
    new_cache_v = jnp.where(hit, new_value[:, :, None, :], moved_v)
    share_heads = query.shape[1] // (kv_heads * head_dim)
    grouped = query.reshape(per_group, kv_heads, share_heads, head_dim)
    scores = (
        jnp.einsum("rkgh,rkph->rkgp", grouped, new_cache_k, preferred_element_type=jnp.float32)
        / head_dim**0.5
    )
    valid = (positions[None, :] <= lengths[:, None])[:, None, None, :]
    scores = jnp.where(valid, scores, jnp.float32(-1e30))
    local_peak = jnp.max(scores, axis=-1)
    values_wide = new_cache_v.astype(jnp.float32)
    weights = jnp.where(valid, jnp.exp(scores - local_peak[..., None]), jnp.float32(0.0))
    local_total = jnp.sum(weights, axis=-1)
    local_context = jnp.einsum(
        "rkgp,rkph->rkgh", weights, values_wide, precision=lax.Precision.HIGHEST
    )
    peak, totals, context = joined((local_peak, local_total, local_context), "dev", merge_states)
    attn = (context / totals[..., None]).reshape(per_group, -1).astype(jnp.bfloat16)
    row_count = out_weight.shape[0]
    attn_mine = lax.dynamic_slice_in_dim(attn, dev_id * row_count, row_count, 1)
    partial_value = jnp.dot(attn_mine, out_weight, preferred_element_type=jnp.float32)
    expert_range = jnp.arange(EXPERTS, dtype=jnp.int32)
    onehot = expert_ids[:, :, None] == expert_range[None, None, :]
    flat_hot = onehot.reshape(per_group * TOP, EXPERTS).astype(jnp.int32)
    before = jnp.cumsum(flat_hot, axis=0) - flat_hot
    route_rank = jnp.sum(before * flat_hot, axis=1).reshape(per_group, TOP)
    slot_hot = (route_rank[:, :, None] == jnp.arange(CAP, dtype=jnp.int32)[None, None, :]).astype(
        jnp.float32
    )
    codes = gate_codes.astype(jnp.float32)
    gate_weight = codes / jnp.sum(codes, axis=-1, keepdims=True)
    selector = jnp.einsum("tke,tkc->ect", onehot.astype(jnp.float32), slot_hot)
    weighted_sel = jnp.einsum("tke,tkc,tk->ect", onehot.astype(jnp.float32), slot_hot, gate_weight)
    col_start = dev_id * feat_width
    split = group_count * dev_count // EXPERTS
    share = lax.psum_scatter(
        partial_value.astype(jnp.bfloat16), "dev", scatter_dimension=1, tiled=True
    ).astype(jnp.float32)
    mixed = resid.astype(jnp.float32) + share
    total_sq = lax.psum(jnp.sum(mixed * mixed, axis=1), "dev")
    gain_mine = lax.dynamic_slice_in_dim(norm_gain, col_start, feat_width).astype(jnp.float32)
    normed = (
        mixed * lax.rsqrt(total_sq / model_width + 1e-05)[:, None] * gain_mine[None, :]
    ).astype(jnp.bfloat16)
    slot_rows = jnp.einsum(
        "ect,tf->ecf", selector.astype(jnp.bfloat16), normed, preferred_element_type=jnp.float32
    ).astype(jnp.bfloat16)
    send_rows = jnp.broadcast_to(slot_rows[:, None], (EXPERTS, split, CAP, feat_width)).reshape(
        group_count * dev_count, CAP, feat_width
    )
    received = lax.all_to_all(send_rows, ("grp", "dev"), split_axis=0, concat_axis=0, tiled=True)
    slot_count = received.shape[1]
    rows = (
        received.reshape(group_count, dev_count, slot_count, feat_width)
        .transpose(0, 2, 1, 3)
        .reshape(group_count * slot_count, model_width)
    )
    outputs = expert_ffn(rows, w_gate, w_up, w_down)
    back = (
        outputs.reshape(group_count, slot_count, dev_count, feat_width)
        .transpose(0, 2, 1, 3)
        .reshape(group_count * dev_count, slot_count, feat_width)
    )
    returned = lax.all_to_all(
        back.astype(jnp.bfloat16), ("grp", "dev"), split_axis=0, concat_axis=0, tiled=True
    ).astype(back.dtype)
    expert_sums = jnp.sum(returned.reshape(EXPERTS, split, CAP, feat_width), axis=1)
    moe = jnp.einsum("ect,ecf->tf", weighted_sel, expert_sums, precision=lax.Precision.HIGHEST)
    layer_out = (mixed + moe).astype(jnp.bfloat16)
    return (new_cache_k, new_cache_v, layer_out)


MESH = pl.DeviceIdType.MESH
BF = jnp.bfloat16
F32 = jnp.float32
SLOTS = 16


def ask(cond):
    return cond.astype(jnp.int32)


def layer_kernel(
    ck_hbm, cv_hbm, source, lengths, query, new_key, new_value, resid, ow_hbm, gain,
    wg_hbm, wu_hbm, wd_hbm, ids_ref, codes_ref,
    nk_hbm, nv_hbm, out_ref,
    ck, cv, rk, rv, sk, sv, nk, nv,
    mask_ref, moved_mask, choose, mc, mr, ms, mt, ws, cs, cr, ss, sr, attn_ref, po, pr, mixed_ref,
    d1s, d1r, d2s, xr, acc_g, acc_u, hid, oacc, r1s, r1r, r2s, r2r, r3s, r3r, wt_ref,
    wbuf, wsem, csem, osem,
    ms_send, ms_recv, ma_send, ma_recv, mb_send, mb_recv, a_send, a_recv, st_send, st_recv, p_send, p_recv,
    e1_send, e1_recv, e2_send, e2_recv, e3_send, e3_recv,
    b1_send, b1_recv, b2_send, b2_recv, b3_send, b3_recv,
):
    G, N = 4, 8
    g = lax.axis_index("grp")
    d = lax.axis_index("dev")
    z, c = d // 2, d % 2
    feat = resid.shape[1]
    width = feat * N
    hidden = wbuf.shape[2]
    block_len = ck.shape[2]

    def grp_peer(i):
        return (lax.rem(g + i, G), d)

    def dev_peer(i):
        return (g, lax.rem(d + i, N))

    def z_peer(i):
        return (g, lax.rem(z + i, 4) * 2 + c)

    sibling = (g, z * 2 + 1 - c)

    def chunk_dev(k):
        other = k // 4
        return lax.rem(z + k % 4, 4) * 2 + c + other * (1 - 2 * c)

    def remote(src, dst, send, recv, to):
        return pltpu.make_async_remote_copy(
            src_ref=src, dst_ref=dst, send_sem=send, recv_sem=recv, device_id=to, device_id_type=MESH
        )

    own_k = pltpu.make_async_copy(ck_hbm, ck, csem.at[0])
    own_v = pltpu.make_async_copy(cv_hbm, cv, csem.at[1])
    own_k.start()
    own_v.start()

    pair = 2 * feat

    def pair_cols(k):
        return pl.ds(pl.multiple_of(lax.rem(z + k, 4) * pair, pair), pair)

    def gate_slot(k):
        return 4 + k

    def up_slot(k):
        return lax.rem(12 + k, SLOTS)

    def down_slot(n):
        return (4 + n // 2) * (1 - n % 2) + lax.rem(12 + n // 2, SLOTS) * (n % 2)

    def load_rows(hbm, k, slot, sem):
        rows = pl.ds(pl.multiple_of(chunk_dev(k) * feat, feat), feat)
        return pltpu.make_async_copy(hbm.at[rows], wbuf.at[slot], wsem.at[sem])

    order = (0, 4, 1, 3, 2, 5, 7, 6)

    def load_gate(p, k):
        return load_rows(wg_hbm, k, gate_slot(p), 4 + p)

    def load_up(p, k):
        return load_rows(wu_hbm, k, up_slot(p), 12 + p)

    def load_out(b):
                return pltpu.make_async_copy(
            ow_hbm.at[:, pair_cols(b + 1)], wbuf.at[b, :, pl.ds(0, pair)], wsem.at[b]
        )

    down_rows = [(0, feat), (feat, feat), (2 * feat, hidden - 2 * feat)]

    def load_down(t, r):
        start, size = down_rows[r]
        n = 3 * t + r
        return pltpu.make_async_copy(
            wd_hbm.at[pl.ds(start, size), pair_cols(t + 1)],
            wbuf.at[down_slot(n), pl.ds(0, size), pl.ds(0, pair)],
            wsem.at[20 + n],
        )

    barrier = pltpu.get_barrier_semaphore()
    for i in range(1, G):
        pl.semaphore_signal(barrier, inc=1, device_id=grp_peer(i), device_id_type=MESH)
    for i in range(1, N):
        pl.semaphore_signal(barrier, inc=1, device_id=dev_peer(i), device_id_type=MESH)
    for b in range(4):
        load_out(b).start()
    for p, k in enumerate(order):
        load_gate(p, k).start()
        if p < 4:
            load_up(p, k).start()

    zero = jnp.int32(0)
    own_k.wait()
    own_v.wait()
    for i in range(1, G):
        q = lax.rem(g + i, G)
        first, second, seen = zero, zero, zero
        for s in range(16):
            v = source[q * 16 + s] - g * 16
            mine = ask(v >= 0) * ask(v < 16)
            first = first + mine * ask(seen == 0) * v
            second = second + mine * ask(seen == 1) * v
            seen = seen + mine
        at = 2 * (i - 1)
        sk[at] = ck[first]
        sk[at + 1] = ck[second]
        sv[at] = cv[first]
        sv[at + 1] = cv[second]

    pl.semaphore_wait(barrier, G - 1 + N - 1)

    moves = []
    for t, (src, dst) in enumerate(((sk, rk), (sv, rv))):
        for i in range(1, G):
            part = pl.ds(2 * (i - 1), 2)
            move = remote(
                src.at[part], dst.at[part], ms_send.at[t, i], ms_recv.at[t, i], grp_peer(i)
            )
            move.start()
            moves.append(move)

    expert_of = lax.broadcasted_iota(jnp.int32, (64, 16), 0) // 8
    slot_of = lax.broadcasted_iota(jnp.int32, (64, 16), 0) % 8
    codes = codes_ref[...].astype(F32)
    total_code = codes[0:1] + codes[1:2]
    hot0 = jnp.where(ids_ref[0:1, :] == expert_of, 1.0, 0.0)
    hot1 = jnp.where(ids_ref[1:2, :] == expert_of, 1.0, 0.0)
    hot = hot0 + hot1
    t_row = lax.broadcasted_iota(jnp.int32, (16, 16), 0)
    t_col = lax.broadcasted_iota(jnp.int32, (16, 16), 1)
    upper = jnp.where(t_row < t_col, 1.0, 0.0).astype(BF)
    rank = jnp.dot(hot.astype(BF), upper, preferred_element_type=F32)
    placed = jnp.where(rank == slot_of.astype(F32), 1.0, 0.0)
    wt_ref[0] = hot * placed
    wt_ref[1] = (hot0 * (codes[0:1] / total_code) + hot1 * (codes[1:2] / total_code)) * placed

    counts = [zero] * G
    p_iota = lax.broadcasted_iota(jnp.int32, (8, block_len, 128), 1)
    places = []
    for s in range(16):
        origin = source[g * 16 + s] // 16
        off = lax.rem(g - origin + G, G)
        at = zero
        for i in range(1, G):
            here = ask(off == i)
            at = at + here * (2 * (i - 1) + counts[i])
            counts[i] = counts[i] + here
        places.append((off, jnp.minimum(at, 5)))

    def insert(own, new, dst):
        for s in range(16):
            hit = p_iota == lengths[s] - d * block_len
            fresh = jnp.broadcast_to(new[s].astype(F32)[:, None, :], (8, block_len, 128))
            dst[s] = jnp.where(hit, fresh, own[s].astype(F32)).astype(BF)

    def iota(shape, axis):
        return lax.broadcasted_iota(jnp.int32, shape, axis)

    columns = 16 * block_len
    lane = iota((96, columns), 1)
    limit = jnp.zeros((96, columns), jnp.int32)
    for s, (off, _) in enumerate(places):
        limit = jnp.where(lane // block_len == s, jnp.where(off == 0, lengths[s], -1), limit)
    inside = (d * block_len + lane % block_len <= limit) & (
        lane // block_len == iota((96, columns), 0) % 16
    )
    mask_ref[...] = jnp.where(inside, 1.0, 0.0)

    holders = []
    for a in range(6):
        holder = jnp.int32(-1)
        for s, (off, at) in enumerate(places):
            holder = holder + ask(off != 0) * ask(at == a) * (s + 1)
        holders.append(holder)

    def held_by(shape):
        place = iota(shape, 0) % 8
        slot = jnp.full(shape, -1, jnp.int32)
        for a, holder in enumerate(holders):
            slot = jnp.where(place == a, holder, slot)
        return slot

    lane = iota((48, columns), 1)
    limit = jnp.zeros((48, columns), jnp.int32)
    for s in range(16):
        limit = jnp.where(lane // block_len == s, lengths[s], limit)
    inside = (d * block_len + lane % block_len <= limit) & (
        lane // block_len == held_by((48, columns))
    )
    moved_mask[...] = jnp.where(inside, 1.0, 0.0)
    chosen = (iota((48, 96), 0) // 8 == iota((48, 96), 1) // 16) & (
        iota((48, 96), 1) % 16 == held_by((48, 96))
    )
    choose[...] = jnp.where(chosen, 1.0, 0.0).astype(BF)

    def build(own, got, new, dst):
        for s, (off, at) in enumerate(places):
            stays = jnp.full((8, block_len, 128), off, jnp.int32) == 0
            hit = p_iota == lengths[s] - d * block_len
            kept = jnp.where(stays, own[s].astype(F32), got[at].astype(F32))
            fresh = jnp.broadcast_to(new[s].astype(F32)[:, None, :], (8, block_len, 128))
            dst[s] = jnp.where(hit, fresh, kept).astype(BF)

    def score(i, moved):
        h = lax.rem(d + i, N)
        rows = [
            query[:, pl.ds(pl.multiple_of((h * 6 + j) * 128, 128), 128)] for j in range(6)
        ]
        q_h = jnp.concatenate(rows, axis=0)
        if moved:
            q_h = jnp.dot(choose[...], q_h, preferred_element_type=F32).astype(BF)
        count = q_h.shape[0]
        k_h = nk[:, pl.ds(h, 1)].reshape(columns, 128)
        valid = (moved_mask if moved else mask_ref)[...] > 0.5
        scores = lax.dot_general(q_h, k_h, (((1,), (1,)), ((), ())), preferred_element_type=F32)
        scores = jnp.where(valid, scores / 128**0.5, F32(-1e30))
        peak = jnp.max(scores, axis=1, keepdims=True)
        weights = jnp.where(valid, jnp.exp(scores - peak), 0.0)
        total = jnp.sum(weights, axis=1, keepdims=True)
        ws[i, 0:count] = weights.astype(BF)
        stat_lane = iota((count, 128), 1)
        stat = jnp.where(stat_lane == 0, peak, jnp.where(stat_lane == 1, total, 0.0))
        stat = jnp.concatenate([stat, jnp.zeros((128 - count, 128), F32)], axis=0)
        (ms if moved else ss)[i] = jnp.transpose(stat)[0:8]

    def score_all(moved):
        def step(m, carry):
            score(2 * m, moved)
            score(2 * m + 1, moved)
            return carry

        lax.fori_loop(0, N // 2, step, 0)

    def send_state(i, moved):
        if moved:
            return (
                remote(mc.at[i], mr.at[i], ma_send.at[i], ma_recv.at[i], dev_peer(i)),
                remote(ms.at[i], mt.at[i], mb_send.at[i], mb_recv.at[i], dev_peer(i)),
            )
        return (
            remote(cs.at[i], cr.at[i], a_send.at[i], a_recv.at[i], dev_peer(i)),
            remote(ss.at[i], sr.at[i], st_send.at[i], st_recv.at[i], dev_peer(i)),
        )

    def attend_all(moved):
        count, out = (48, mc) if moved else (96, cs)
        for i in (*range(1, N), 0):
            v_h = nv[:, pl.ds(lax.rem(d + i, N), 1)].reshape(columns, 128)
            out[i] = jnp.dot(ws[i, 0:count], v_h, preferred_element_type=F32).astype(BF)
            if i:
                for copy in send_state(i, moved):
                    copy.start()

    def merged(moved):
        count, parts, stats = (48, mr, mt) if moved else (96, cr, sr)
        for i in range(1, N):
            for copy in send_state(i, moved):
                copy.wait_recv()
        peaks = jnp.concatenate([stats[i, 0:1] for i in range(N)], axis=0)
        totals = jnp.concatenate([stats[i, 1:2] for i in range(N)], axis=0)
        scale = jnp.exp(peaks - jnp.max(peaks, axis=0, keepdims=True))
        norm = jnp.sum(scale * totals, axis=0, keepdims=True)
        norm = jnp.where(norm > 0.0, norm, 1.0)
        factor = jnp.concatenate([scale / norm, jnp.zeros((120, 128), F32)], axis=0)
        factor = jnp.transpose(factor)
        context = jnp.zeros((count, 128), F32)
        for i in range(N):
            context = context + parts[i].astype(F32) * factor[0:count, i : i + 1]
        return context

    insert(ck, new_key, nk)
    insert(cv, new_value, nv)
    score_all(False)
    attend_all(False)
    cr[0] = cs[0]
    sr[0] = ss[0]

    for move in moves[: G - 1]:
        move.wait_recv()
    build(ck, rk, new_key, nk)
    put_k = pltpu.make_async_copy(nk, nk_hbm, osem.at[0])
    put_v = pltpu.make_async_copy(nv, nv_hbm, osem.at[1])
    put_k.start()
    score_all(True)
    for move in moves[G - 1 :]:
        move.wait_recv()
    build(cv, rv, new_value, nv)
    put_v.start()
    attend_all(True)
    mr[0] = mc[0]
    mt[0] = ms[0]
    context = merged(False)
    arrived = merged(True).astype(BF)
    context = context + lax.dot_general(
        choose[...], arrived, (((0,), (0,)), ((), ())), preferred_element_type=F32
    )
    for j in range(6):
        attn_ref[:, j * 128 : (j + 1) * 128] = context[j * 16 : (j + 1) * 16].astype(BF)

    def feat_cols(j):
        return pl.ds(pl.multiple_of(j * feat, feat), feat)

    def send_partial(k, core):
        at = 2 * k + core
        return remote(
            po.at[k, :, feat_cols(core)],
            pr.at[2 * k + c],
            p_send.at[at],
            p_recv.at[2 * k + c],
            (g, lax.rem(z + k, 4) * 2 + core),
        )

    def core_partial():
        return remote(po.at[0, :, feat_cols(1 - c)], pr.at[0], p_send.at[0], p_recv.at[0], sibling)

    for b in range(4):
        load_out(b).wait()
        k = (b + 1) % 4
        value = jnp.dot(
            attn_ref[...], wbuf[b, :, 0:pair], preferred_element_type=F32
        )
        po[k] = value.astype(BF)
        if k:
            send_partial(k, 0).start()
            send_partial(k, 1).start()
        else:
            core_partial().start()
    for p in range(4, 8):
        load_up(p, order[p]).start()

    mixed = resid[...].astype(F32) + po[0, :, feat_cols(c)].astype(F32)
    core_partial().wait_recv()
    mixed = mixed + pr[0].astype(F32)
    for at in range(2, N):
        remote(
            po.at[0, :, feat_cols(0)], pr.at[at], p_send.at[1], p_recv.at[at], sibling
        ).wait_recv()
        mixed = mixed + pr[at].astype(F32)
    mixed_ref[...] = mixed

    square = jnp.sum(mixed * mixed, axis=1, keepdims=True)
    high = square.astype(BF).astype(F32)
    tail_lane = lax.broadcasted_iota(jnp.int32, (16, 128), 1)
    tail = jnp.where(tail_lane == 0, high, jnp.where(tail_lane == 1, square - high, 0.0))
    scaled = mixed * gain[feat_cols(d)].astype(F32).reshape(1, feat)
    ext = jnp.concatenate([scaled, tail], axis=1).astype(BF)
    routed = lax.dot_general(
        wt_ref[0].astype(BF), ext, (((1,), (0,)), ((), ())), preferred_element_type=F32
    ).astype(BF)
    for q in range(G):
        d1s[q] = routed[q * 16 : (q + 1) * 16]

    def send_routed(i):
        return remote(
            d1s.at[lax.rem(g + i, G)], d1r.at[g], e1_send.at[i], e1_recv.at[i], grp_peer(i)
        )

    for i in range(1, G):
        send_routed(i).start()
    d1r[g] = d1s[g]
    for i in range(1, G):
        send_routed(i).wait_recv()
    arrived = [d1r[q].astype(F32) for q in range(G)]
    for e in range(2):
        d2s[e] = jnp.concatenate([a[e * 8 : (e + 1) * 8] for a in arrived], axis=0).astype(BF)

    def send_rows(i):
        return remote(
            d2s.at[lax.rem(z + i, 4) // 2], xr.at[4 - i], e2_send.at[4 - i], e2_recv.at[4 - i], z_peer(i)
        )

    def send_core(k):
        return remote(xr.at[k], xr.at[4 + k], e3_send.at[k], e3_recv.at[k], sibling)

    for i in (2, 1, 3):
        send_rows(i).start()
    xr[0] = d2s[z // 2]
    send_core(0).start()

    acc_g[...] = jnp.zeros(acc_g.shape, F32)
    acc_u[...] = jnp.zeros(acc_u.shape, F32)

    def feed_two(p, first, second):
        def feed(n, carry):
            k = first + n * (second - first)
            load_gate(p + n, k).wait()
            load_up(p + n, k).wait()
            rows = xr[k, :, 0:feat]
            acc_g[...] += jnp.dot(rows, wbuf[gate_slot(p + n)], preferred_element_type=F32)
            acc_u[...] += jnp.dot(rows, wbuf[up_slot(p + n)], preferred_element_type=F32)
            return carry

        lax.fori_loop(0, 2, feed, 0)
        if p < 6:
            for n in range(2 * p, 2 * p + 4):
                load_down(n // 3, n % 3).start()

    send_core(0).wait_recv()
    feed_two(0, 0, 4)
    for k in (1, 3):
        send_rows(4 - k).wait_recv()
        send_core(k).start()
    feed_two(2, 1, 3)
    send_rows(2).wait_recv()
    send_core(2).start()
    send_core(1).wait_recv()
    feed_two(4, 2, 5)
    send_core(3).wait_recv()
    send_core(2).wait_recv()
    feed_two(6, 7, 6)

    squares = jnp.zeros((32, 1), F32)
    for k in range(8):
        squares = squares + jnp.sum(xr[k, :, feat:].astype(F32), axis=1, keepdims=True)
    inv = lax.rsqrt(squares / width + 1e-05)
    gate_val = acc_g[...] * inv
    hid[...] = (gate_val / (1.0 + jnp.exp(-gate_val)) * (acc_u[...] * inv)).astype(BF)

    def back_core(k):
        return remote(r1s.at[k], r1r.at[k], b1_send.at[k], b1_recv.at[k], sibling)

    def back_rows(k):
        return remote(r2s.at[k], r2r.at[k], b2_send.at[k], b2_recv.at[k], z_peer(k + 1))

    def back_group(i):
        return remote(
            r3s.at[lax.rem(g + i, G)], r3r.at[g], b3_send.at[i], b3_recv.at[i], grp_peer(i)
        )

    def expand(t):
        value = jnp.zeros((32, pair), F32)
        for r, (start, size) in enumerate(down_rows):
            load_down(t, r).wait()
            value = value + jnp.dot(
                hid[:, start : start + size],
                wbuf[down_slot(3 * t + r), 0:size, 0:pair],
                preferred_element_type=F32,
            )
        oacc[t] = value
        r1s[t] = oacc[t, :, feat_cols(1 - c)].astype(BF)
        back_core(t).start()

    def joined_share(t):
        back_core(t).wait_recv()
        return oacc[t, :, feat_cols(c)] + r1r[t].astype(F32)

    def expand_step(t, carry):
        expand(t)
        r2s[t - 1] = joined_share(t - 1).astype(BF)
        back_rows(t - 1).start()
        return carry

    expand(0)
    lax.fori_loop(1, 4, expand_step, 0)
    value = joined_share(3)
    even_share = 1.0 - (z // 2).astype(F32)
    even = value * even_share
    odd = value * (1.0 - even_share)
    for t in range(3):
        back_rows(t).wait_recv()
        share = 1.0 - (lax.rem(z - t + 3, 4) // 2).astype(F32)
        value = r2r[t].astype(F32)
        even = even + value * share
        odd = odd + value * (1.0 - share)
    for q in range(G):
        r3s[q] = jnp.concatenate([even[q * 8 : q * 8 + 8], odd[q * 8 : q * 8 + 8]], axis=0).astype(BF)
    for i in range(1, G):
        back_group(i).start()
    r3r[g] = r3s[g]
    for i in range(1, G):
        back_group(i).wait_recv()
    rows = jnp.concatenate([r3r[q] for q in range(G)], axis=0)
    wt_high = wt_ref[1].astype(BF)
    wt_low = (wt_ref[1] - wt_high.astype(F32)).astype(BF)
    moe = sum(
        lax.dot_general(part, rows, (((0,), (0,)), ((), ())), preferred_element_type=F32)
        for part in (wt_high, wt_low)
    )
    out_ref[...] = (mixed_ref[...] + moe).astype(BF)

    put_k.wait()
    put_v.wait()
    for move in moves:
        move.wait_send()
    for i in range(1, N):
        for copy in (*send_state(i, False), *send_state(i, True)):
            copy.wait_send()
    core_partial().wait_send()
    for k in range(1, 4):
        send_partial(k, 0).wait_send()
        send_partial(k, 1).wait_send()
    for i in range(1, G):
        send_routed(i).wait_send()
        send_rows(i).wait_send()
        back_rows(i - 1).wait_send()
        back_group(i).wait_send()
    for k in range(4):
        send_core(k).wait_send()
        back_core(k).wait_send()


def hand_over(k_in, v_in, out_in, k_out, v_out, out_out, k_mid, v_mid, out_mid, in_sems, out_sems):
    stages = [(out_in, out_mid, out_out)]
    quarter = k_in.shape[0] // 4
    for n in range(4):
        part = pl.ds(n * quarter, quarter)
        stages.append((k_in.at[part], k_mid.at[part], k_out.at[part]))
        stages.append((v_in.at[part], v_mid.at[part], v_out.at[part]))
    first = [
        pltpu.make_async_copy(src, mid, in_sems.at[n]) for n, (src, mid, _) in enumerate(stages)
    ]
    second = [
        pltpu.make_async_copy(mid, dst, out_sems.at[n]) for n, (_, mid, dst) in enumerate(stages)
    ]
    for copy in first:
        copy.start()
    for came, goes in zip(first, second):
        came.wait()
        goes.start()
    for copy in second:
        copy.wait()


def fused_layer(
    cache_k, cache_v, source, lengths, query, new_key, new_value, resid, out_weight, norm_gain,
    w_gate, w_up, w_down, expert_ids, gate_codes,
):
    feat = resid.shape[1]
    width = query.shape[1]
    hidden = w_gate.shape[1]
    ext = feat + 128
    block = cache_k.shape[1:]
    vm = pl.BlockSpec(memory_space=pltpu.VMEM)
    sm = pl.BlockSpec(memory_space=pltpu.SMEM)
    far = pl.BlockSpec(memory_space=pl.ANY)
    dma = pltpu.SemaphoreType.DMA

    def buf(shape, kind=BF):
        return pltpu.VMEM(shape, kind)

    scratch = [
        buf((16, *block)), buf((16, *block)), buf((6, *block)), buf((6, *block)),
        buf((6, *block)), buf((6, *block)), buf((16, *block)), buf((16, *block)),
        buf((96, 16 * block[1]), F32),
        buf((48, 16 * block[1]), F32), buf((48, 96)), buf((8, 48, 128)), buf((8, 48, 128)),
        buf((8, 8, 128), F32), buf((8, 8, 128), F32), buf((8, 96, 16 * block[1])), buf((8, 96, 128)), buf((8, 96, 128)),
        buf((8, 8, 128), F32), buf((8, 8, 128), F32), buf((16, feat)), buf((4, 16, 2 * feat)),
        buf((8, 16, feat)), buf((16, feat), F32),
        buf((4, 16, ext)), buf((4, 16, ext)), buf((2, 32, ext)), buf((8, 32, ext)),
        buf((32, hidden), F32), buf((32, hidden), F32), buf((32, hidden)), buf((4, 32, 2 * feat), F32),
        buf((4, 32, feat)), buf((4, 32, feat)), buf((4, 32, feat)), buf((4, 32, feat)),
        buf((4, 16, feat)), buf((4, 16, feat)), buf((2, 64, 16), F32),
        buf((SLOTS, feat, hidden)), dma((32,)), dma((2,)), dma((2,)),
        dma((2, 4)), dma((2, 4)), dma((8,)), dma((8,)), dma((8,)), dma((8,)), dma((8,)), dma((8,)), dma((8,)), dma((8,)), dma((8,)), dma((8,)),
        dma((4,)), dma((4,)), dma((4,)), dma((4,)), dma((4,)), dma((4,)),
        dma((4,)), dma((4,)), dma((4,)), dma((4,)), dma((4,)), dma((4,)),
    ]
    results = pl.pallas_call(
        layer_kernel,
        out_shape=(
            jax.ShapeDtypeStruct(cache_k.shape, BF),
            jax.ShapeDtypeStruct(cache_v.shape, BF),
            jax.ShapeDtypeStruct(resid.shape, BF),
        ),
        in_specs=[far, far, sm, sm, vm, vm, vm, vm, far, vm, far, far, far, vm, vm],
        out_specs=(far, far, vm),
        scratch_shapes=scratch,
        compiler_params=pltpu.CompilerParams(
            collective_id=0, has_side_effects=True, vmem_limit_bytes=(64 << 20) - (256 << 10)
        ),
        cost_estimate=pl.CostEstimate(
            flops=2 * 32 * 3 * width * hidden, bytes_accessed=6 * width * hidden, transcendentals=0
        ),
    )(
        cache_k, cache_v, source, lengths, query, new_key, new_value, resid, out_weight,
        norm_gain, w_gate, w_up, w_down, expert_ids.T, gate_codes.T,
    )
    return pl.pallas_call(
        hand_over,
        out_shape=tuple(jax.ShapeDtypeStruct(r.shape, r.dtype) for r in results),
        in_specs=[far] * 3,
        out_specs=(far,) * 3,
        scratch_shapes=[buf(r.shape) for r in results] + [dma((9,)), dma((9,))],
        cost_estimate=pl.CostEstimate(flops=0, bytes_accessed=8 << 20, transcendentals=0),
    )(*results)


def device_program(*args):
    cache_k, query, resid, w_gate = args[0], args[4], args[7], args[10]
    fits = (
        lax.axis_size("grp") == 4
        and lax.axis_size("dev") == cache_k.shape[1]
        and resid.shape[1] * lax.axis_size("dev") == query.shape[1]
        and w_gate.shape[1] * 3 == query.shape[1]
        and cache_k.shape[0] == 16
    )
    return fused_layer(*args) if fits else on_device(*args)


def solution(mesh):
    in_specs = (
        P("grp", None, "dev", None),
        P("grp", None, "dev", None),
        P(),
        P("grp"),
        P("grp", None),
        P("grp", None, None),
        P("grp", None, None),
        P("grp", "dev"),
        P("dev", None),
        P(),
        P(None, ("grp", "dev")),
        P(None, ("grp", "dev")),
        P(("grp", "dev"), None),
        P("grp", None),
        P("grp", None),
    )
    out_specs = (P("grp", None, "dev", None), P("grp", None, "dev", None), P("grp", "dev"))
    return jax.shard_map(
        device_program, mesh=mesh, in_specs=in_specs, out_specs=out_specs, check_vma=False
    )
```
